32 devices in a mesh: groups: 2 (over y), state: 4 (over z), obs: 2 (over x), cores: 2 (over core).
Axes of the slice: x: 2, y: 2, z: 4, core: 2. Of those that a mesh axis runs over, the one named last changes fastest.
Arguments:
- ensemble: float32 [128, 128, 512], P(('groups', 'state'), ('obs', 'cores')), parts along dimension 0, may hold values from -6 to 6
- obs_value: float32 [2048], P('groups'), parts along dimension 0, may hold values from -8 to 8
- obs_var: float32 [2048], P('groups'), parts along dimension 0, may hold values from 0.25 to 4
- obs_cell: int32 [2048], P('groups'), parts along dimension 0, may hold values from 0 to 65535, as said below
- obs_order: int32 [2048], P('groups'), parts along dimension 0, may hold values from 0 to 1023, each once
- obs_blocks: int32 [2048, 6], P('groups'), parts along dimension 0, may hold values from 0 to 15, as said below
Outputs:
- posterior: float32 [128, 128, 512], P(('groups', 'state'), ('obs', 'cores')), parts along dimension 0
The draws below stay inside these ranges and needn't reach their ends.
There are 2 independent parts, one for each index of `groups`. The reference program is written for one: setup_inputs(seed, part) draws one part's arguments, and reference() takes and returns one part's arrays. A program takes and returns all parts, laid end to end along the dimension named above; each array names one. Nothing has to cross between parts.
Inputs may be any that keep to these rules, and one draw needn't show every extreme that they name: `obs_cell`: each entry is the index row * 512 + column of a slab cell; observations gather around a few points of the slab. `obs_order`: every observation appears once. `obs_blocks`: row k holds 6 distinct blocks: first the block of observation k's cell, then the block in the same row band whose column band lies 4 // 2 bands away, then blocks whose row band and column band each differ from the first by at most one, cyclically.
All inputs are finite; a program needn't handle non-finite values.
Results may differ from the reference program's by a relative error of at most 0.0003.
Values sent between devices are 32-bit elements; how exact they have to be, the bound alone decides.
A program may use at most 64 MiB of HBM per device.

```python
import math
import jax
import jax.numpy as jnp
from jax import lax

M = 64
ROWS_DEV = 32
COLS_DEV = 128
BATCHES = 4
BATCH_OBS = 256
LIST = 6
NOBS = 1024
NBR = 4
NBC = 4
BLOCKS = 16
ROWS = 128
COLS = 512


def obs_layout(key):
    base = jax.random.fold_in(key, 7)
    keys = jax.random.split(base, 9)
    centre_row = jax.random.randint(keys[0], (4,), 0, ROWS)
    centre_col = jax.random.randint(keys[1], (4,), 0, COLS)
    cluster = jax.random.randint(keys[2], (NOBS,), 0, 4)
    spread_out = jax.random.randint(keys[3], (NOBS,), 0, 2)
    near_row = (centre_row[cluster] + jax.random.randint(keys[4], (NOBS,), -ROWS_DEV, ROWS_DEV + 1)) % ROWS
    near_col = (centre_col[cluster] + jax.random.randint(keys[5], (NOBS,), -COLS_DEV, COLS_DEV + 1)) % COLS
    free_row = jax.random.randint(keys[6], (NOBS,), 0, ROWS)
    free_col = jax.random.randint(keys[7], (NOBS,), 0, COLS)
    obs_row = jnp.where(spread_out == 1, free_row, near_row)
    obs_col = jnp.where(spread_out == 1, free_col, near_col)
    cells = (obs_row * COLS + obs_col).astype(jnp.int32)
    band_row = obs_row // ROWS_DEV
    band_col = obs_col // COLS_DEV
    row_offset = jnp.array([-1, -1, -1, 0, 0, 1, 1, 1], dtype=jnp.int32)
    col_offset = jnp.array([-1, 0, 1, -1, 1, -1, 0, 1], dtype=jnp.int32)
    scores = jax.random.randint(keys[8], (NOBS, 8), 0, 2 ** 20) * 8 + jnp.arange(8, dtype=jnp.int32)[None, :]
    picked = jnp.argsort(scores, axis=1)[:, :LIST - 2]
    near_rows = (band_row[:, None] + row_offset[picked]) % NBR
    near_cols = (band_col[:, None] + col_offset[picked]) % NBC
    own_block = (band_row * NBC + band_col)[:, None]
    far_block = (band_row * NBC + (band_col + NBC // 2) % NBC)[:, None]
    blocks = jnp.concatenate([own_block, far_block, near_rows * NBC + near_cols], axis=1).astype(jnp.int32)
    return (cells, blocks)


def draw_obs_cell(key, part):
    return obs_layout(key)[0]


def draw_obs_blocks(key, part):
    return obs_layout(key)[1]


def steps_of(own_key, dims, shards, low, top_value):
    loudness, own = 1.0, jax.random.fold_in(own_key, 6)
    for axis_at, blocks in shards:
        steps = jnp.exp(jax.random.uniform(jax.random.fold_in(own, axis_at), (blocks,), jnp.float32, low / len(shards), top_value / len(shards)))
        loudness = loudness * jnp.repeat(steps, dims[axis_at] // blocks).reshape([-1 if axis == axis_at else 1 for axis in range(len(dims))])
    return loudness


def bell_draw(rng, extent, deviation, most, shards=(), kind=jnp.bfloat16):
    entries = jax.random.normal(rng, extent, jnp.float32) * deviation
    if len(shards) > 0:
        entries = steps_of(rng, extent, shards, -0.22, 0.18) * entries
    return jnp.clip(entries, min=-most, max=most).astype(kind)


def setup_inputs(seed: int = 0, part: int = 0) -> dict:
    splits = jax.random.split(jax.random.key(seed), 7)
    part_splits = jax.random.split(jax.random.fold_in(splits[6], part), 7)
    ensemble = bell_draw(part_splits[0], (M, ROWS, COLS), 1.0, 6.0, ((0, 4), (1, 4)), jnp.float32)
    obs_value = bell_draw(part_splits[1], (NOBS,), 1.5, 8.0, (), jnp.float32)
    obs_var = jnp.clip(jnp.exp(jax.random.uniform(part_splits[2], (NOBS,), jnp.float32, math.log(0.25), math.log(4.0))), 0.25, 4.0)
    obs_cell = draw_obs_cell(jax.random.fold_in(jax.random.fold_in(splits[6], part), 71), part)
    obs_order = jax.random.permutation(part_splits[4], NOBS).astype(jnp.int32)
    obs_blocks = draw_obs_blocks(jax.random.fold_in(jax.random.fold_in(splits[6], part), 71), part)
    return {"ensemble": ensemble, "obs_value": obs_value, "obs_var": obs_var, "obs_cell": obs_cell, "obs_order": obs_order, "obs_blocks": obs_blocks}


def adjust_obs(prior_ens, obs_value, obs_var):
    members = prior_ens.shape[1]
    ens_mean = lax.optimization_barrier(jnp.mean(prior_ens, axis=1))
    obs_anom = prior_ens - ens_mean[:, None]
    obs_spread = lax.optimization_barrier(jnp.sum(obs_anom * obs_anom, axis=1)) / (members - 1) + 1e-06
    post_var = 1.0 / (1.0 / obs_spread + 1.0 / obs_var)
    post_mean = post_var * (ens_mean / obs_spread + obs_value / obs_var)
    shrink = jnp.sqrt(post_var / obs_spread)
    obs_step = post_mean[:, None] + shrink[:, None] * obs_anom - prior_ens
    return (obs_anom, obs_step, obs_spread)

def reference(ensemble, obs_value, obs_var, obs_cell, obs_order, obs_blocks):
    fields = ensemble
    block_ids = jnp.arange(BLOCKS, dtype=jnp.int32)
    for batch in range(BATCHES):
        obs_ids = obs_order[batch * BATCH_OBS:(batch + 1) * BATCH_OBS]
        obs_cells = obs_cell[obs_ids]
        flat_fields = fields.reshape(M, ROWS * COLS)
        prior_ens = flat_fields[:, obs_cells].T
        obs_anom, obs_step, obs_spread = adjust_obs(prior_ens, obs_value[obs_ids], obs_var[obs_ids])
        obs_row = obs_cells // COLS
        obs_col = obs_cells % COLS
        lists = obs_blocks[obs_ids]
        blockmask = jnp.any(lists[:, :, None] == block_ids[None, None, :], axis=1).astype(jnp.float32)
        stacked = fields.reshape(M, NBR, ROWS_DEV, COLS).transpose(1, 0, 2, 3)

        def one_block(pair):
            block_piece, row_band = pair
            cell_row = row_band * ROWS_DEV + jnp.arange(ROWS_DEV, dtype=jnp.int32)
            cell_col = jnp.arange(COLS, dtype=jnp.int32)
            row_gap = jnp.abs(cell_row[None, :] - obs_row[:, None])
            row_gap = jnp.minimum(row_gap, ROWS - row_gap)
            col_gap = jnp.abs(cell_col[None, :] - obs_col[:, None])
            col_gap = jnp.minimum(col_gap, COLS - col_gap)
            row_term = (4.0 * row_gap.astype(jnp.float32) / ROWS) ** 2
            col_term = (4.0 * col_gap.astype(jnp.float32) / COLS) ** 2
            taper_weight = jnp.exp(-0.5 * (row_term[:, :, None] + col_term[:, None, :]))
            start_col = (row_band * NBC).astype(jnp.int32)
            band_mask = lax.dynamic_slice(blockmask, (jnp.zeros((), jnp.int32), start_col), (BATCH_OBS, NBC))
            listed = jnp.repeat(band_mask, COLS_DEV, axis=1)
            taper_mask = taper_weight * listed[:, None, :]
            anomaly = block_piece - lax.optimization_barrier(jnp.mean(block_piece, axis=0))
            covariance = jnp.einsum('km,mrc->krc', obs_anom, anomaly, precision=lax.Precision.HIGHEST) / (M - 1)
            regression = covariance * taper_mask / obs_spread[:, None, None]
            return block_piece + jnp.einsum('km,krc->mrc', obs_step, regression, precision=lax.Precision.HIGHEST)
        updated = lax.map(one_block, (stacked, jnp.arange(NBR, dtype=jnp.int32)))
        fields = updated.transpose(1, 0, 2, 3).reshape(M, ROWS, COLS)
    return fields
```

```python
import jax
import jax.numpy as jnp
from jax import lax
from jax.sharding import PartitionSpec as P

BATCHES = 4
BATCH_OBS = 256


def adjust_obs(prior_ens, obs_value, obs_var):
    members = prior_ens.shape[1]
    ens_mean = jnp.mean(prior_ens, axis=1)
    obs_anom = prior_ens - ens_mean[:, None]
    obs_spread = jnp.sum(obs_anom * obs_anom, axis=1) / (members - 1) + 1e-06
    post_var = 1.0 / (1.0 / obs_spread + 1.0 / obs_var)
    post_mean = post_var * (ens_mean / obs_spread + obs_value / obs_var)
    shrink = jnp.sqrt(post_var / obs_spread)
    obs_step = post_mean[:, None] + shrink[:, None] * obs_anom - prior_ens
    return (obs_anom, obs_step, obs_spread)


def distance_taper(obs_row, obs_col, cell_row, cell_col, rows_all, cols_all):
    row_gap = jnp.abs(cell_row[None, :] - obs_row[:, None])
    row_gap = jnp.minimum(row_gap, rows_all - row_gap)
    col_gap = jnp.abs(cell_col[None, :] - obs_col[:, None])
    col_gap = jnp.minimum(col_gap, cols_all - col_gap)
    row_term = (4.0 * row_gap.astype(jnp.float32) / rows_all) ** 2
    col_term = (4.0 * col_gap.astype(jnp.float32) / cols_all) ** 2
    return jnp.exp(-0.5 * (row_term + col_term))


def on_device(ensemble, obs_value, obs_var, obs_cell, obs_order, obs_blocks):
    n_state = lax.axis_size("state")
    n_obs = lax.axis_size("obs")
    n_cores = lax.axis_size("cores")
    mem_dev, row_dev, cols_all = ensemble.shape
    members = mem_dev * n_state
    col_dev = cols_all // n_state
    rows_all = row_dev * n_obs * n_cores
    row_band = lax.axis_index("obs") * n_cores + lax.axis_index("cores")
    row_start = row_band * row_dev
    col_start = lax.axis_index("state") * col_dev
    nobs = obs_order.shape[0]

    table = jnp.concatenate(
        [
            obs_value[:, None],
            obs_var[:, None],
            obs_cell.astype(jnp.float32)[:, None],
            obs_blocks.astype(jnp.float32),
        ],
        axis=1,
    )[obs_order]
    value, var = table[:, 0], table[:, 1]
    cells = table[:, 2].astype(jnp.int32)
    lists = table[:, 3:].astype(jnp.int32)
    obs_row = cells // cols_all
    obs_col = cells % cols_all
    obs_block = (obs_row // row_dev) * n_state + obs_col // col_dev

    owned = (obs_row >= row_start) & (obs_row < row_start + row_dev)
    index = jnp.clip((obs_row - row_start) * cols_all + obs_col, 0, row_dev * cols_all - 1)
    mine = jnp.where(owned[None, :], ensemble.reshape(mem_dev, row_dev * cols_all)[:, index], 0.0)
    slot = jnp.zeros((members, nobs), jnp.float32)
    slot = lax.dynamic_update_slice_in_dim(slot, mine, lax.axis_index("state") * mem_dev, 0)
    at_obs = lax.psum(slot, ("state", "obs", "cores"))

    local_fields = lax.all_to_all(ensemble, "state", split_axis=2, concat_axis=0, tiled=True)
    count = row_dev * col_dev
    flat_index = jnp.arange(count, dtype=jnp.int32)
    cell_row = jnp.concatenate([row_start + flat_index // col_dev, obs_row])
    cell_col = jnp.concatenate([col_start + flat_index % col_dev, obs_col])
    my_block = row_band * n_state + lax.axis_index("state")
    cell_block = jnp.concatenate([jnp.full((count,), my_block, jnp.int32), obs_block])
    fields = jnp.concatenate([local_fields.reshape(members, count), at_obs], axis=1)
    for batch in range(BATCHES):
        part = slice(batch * BATCH_OBS, (batch + 1) * BATCH_OBS)
        prior_ens = fields[:, count + batch * BATCH_OBS : count + (batch + 1) * BATCH_OBS].T
        obs_anom, obs_step, obs_spread = adjust_obs(prior_ens, value[part], var[part])
        keep = count + nobs if batch < BATCHES - 1 else count
        listed = jnp.any(lists[part][:, :, None] == cell_block[None, None, :keep], axis=1)
        taper = distance_taper(
            obs_row[part], obs_col[part], cell_row[:keep], cell_col[:keep], rows_all, cols_all
        )
        taper_mask = jnp.where(listed, taper, 0.0)
        fields = fields[:, :keep]
        anomaly = fields - jnp.mean(fields, axis=0)
        covariance = jnp.dot(obs_anom, anomaly, precision=lax.Precision.HIGHEST) / (members - 1)
        regression = covariance * taper_mask / obs_spread[:, None]
        fields = fields + jnp.dot(obs_step.T, regression, precision=lax.Precision.HIGHEST)
    out_fields = fields.reshape(members, row_dev, col_dev)
    return lax.all_to_all(out_fields, "state", split_axis=0, concat_axis=2, tiled=True)


def solution(mesh):
    placed = (
        P(("groups", "state"), ("obs", "cores"), None),
        P("groups"),
        P("groups"),
        P("groups"),
        P("groups"),
        P("groups", None),
    )
    return jax.shard_map(
        on_device,
        mesh=mesh,
        in_specs=placed,
        out_specs=P(("groups", "state"), ("obs", "cores"), None),
        check_vma=False,
    )
```

```python
import functools
import jax
import jax.numpy as jnp
from jax import lax
from jax.experimental import pallas as pl
from jax.experimental.pallas import tpu as pltpu
from jax.sharding import PartitionSpec as P

BATCHES = 4
BATCH_OBS = 256
CHUNKS = 4


def adjust_obs(prior_ens, obs_value, obs_var):
    members = prior_ens.shape[1]
    ens_mean = jnp.mean(prior_ens, axis=1)
    obs_anom = prior_ens - ens_mean[:, None]
    obs_spread = jnp.sum(obs_anom * obs_anom, axis=1) / (members - 1) + 1e-06
    post_var = 1.0 / (1.0 / obs_spread + 1.0 / obs_var)
    post_mean = post_var * (ens_mean / obs_spread + obs_value / obs_var)
    shrink = jnp.sqrt(post_var / obs_spread)
    obs_step = post_mean[:, None] + shrink[:, None] * obs_anom - prior_ens
    return (obs_anom, obs_step, obs_spread)


def distance_taper(obs_row, obs_col, cell_row, cell_col, rows_all, cols_all):
    row_gap = jnp.abs(cell_row[None, :] - obs_row[:, None])
    row_gap = jnp.minimum(row_gap, rows_all - row_gap)
    col_gap = jnp.abs(cell_col[None, :] - obs_col[:, None])
    col_gap = jnp.minimum(col_gap, cols_all - col_gap)
    row_term = (4.0 * row_gap.astype(jnp.float32) / rows_all) ** 2
    col_term = (4.0 * col_gap.astype(jnp.float32) / cols_all) ** 2
    return jnp.exp(-0.5 * (row_term + col_term))


def halves(x):
    high = x.astype(jnp.bfloat16)
    return high, (x - high.astype(jnp.float32)).astype(jnp.bfloat16)


def dot32(a, b):
    return jnp.dot(a, b, preferred_element_type=jnp.float32)


def gap_weight(a, b, extent):
    gap = jnp.abs(a - b)
    gap = jnp.minimum(gap, extent - gap)
    term = gap * (4.0 / extent)
    return jnp.exp(-0.5 * (term * term))


def split_anomaly(x):
    high, low = halves(x - jnp.mean(x, axis=0, keepdims=True))
    return jnp.concatenate([high, low, high], axis=0)


def kernel(n_state, n_cores, n_list, ens, lanes, subs, out, turned, fld, back, part, prior,
           anom3, step, row_w, col_w, pair_w, s1, r1, s2, r2, s3, r3, s_in, r_in, s_out, r_out):
    mem_dev, row_dev, cols_all = ens.shape
    bands = BATCHES
    rows_all = row_dev * bands
    col_dev = cols_all // n_state
    members = mem_dev * n_state
    z = lax.axis_index("state")
    band = lax.axis_index("obs") * n_cores + lax.axis_index("cores")
    rows_chunk = row_dev // CHUNKS
    f32 = jnp.float32

    def z_peer(i):
        return lax.rem(z + i, n_state)

    def band_peer(i):
        p = lax.rem(band + i, bands)
        return {"obs": p // n_cores, "cores": lax.rem(p, n_cores)}, p

    def remote(src, dst, send, recv, device):
        return pltpu.make_async_remote_copy(
            src_ref=src, dst_ref=dst, send_sem=send, recv_sem=recv,
            device_id=device, device_id_type=pl.DeviceIdType.MESH,
        )

    barrier = pltpu.get_barrier_semaphore()
    for i in range(1, n_state):
        pl.semaphore_signal(barrier, inc=1, device_id={"state": z_peer(i)}, device_id_type=pl.DeviceIdType.MESH)
    for i in range(1, bands):
        pl.semaphore_signal(barrier, inc=1, device_id=band_peer(i)[0], device_id_type=pl.DeviceIdType.MESH)

    flat = ens[...].reshape(mem_dev * row_dev, cols_all)
    high = flat.astype(jnp.bfloat16)
    rest = flat - high.astype(f32)
    mid = rest.astype(jnp.bfloat16)
    low = (rest - mid.astype(f32)).astype(jnp.bfloat16)
    col_iota = lax.broadcasted_iota(jnp.int32, (cols_all, BATCH_OBS), 0).astype(f32)
    row_iota = lax.broadcasted_iota(jnp.int32, (row_dev, BATCH_OBS), 0).astype(f32) + (band * row_dev).astype(f32)
    for b in range(BATCHES):
        o = pl.ds(b * BATCH_OBS, BATCH_OBS)
        onehot = jnp.where(col_iota == lanes[3:4, o], 1.0, 0.0).astype(jnp.bfloat16)
        picked = (dot32(low, onehot) + dot32(mid, onehot)) + dot32(high, onehot)
        mask = row_iota == lanes[2:3, o]
        picked = jnp.where(mask[None], picked.reshape(mem_dev, row_dev, BATCH_OBS), 0.0)
        turned_part = jnp.sum(picked, axis=1)
        part[bands + b] = turned_part

    pl.semaphore_wait(barrier, n_state - 1 + bands - 1)

    first = []
    for i in range(1, bands):
        device, p = band_peer(i)
        first.append(remote(part.at[bands + p], part.at[i], s1.at[i], r1.at[i], device))
        first[-1].start()
    for i in range(n_state):
        d = z_peer(i)
        piece = jnp.swapaxes(ens[:, :, pl.ds(pl.multiple_of(d * col_dev, col_dev), col_dev)], 0, 1)
        if i == 0:
            fld[:, pl.ds(pl.multiple_of(z * mem_dev, mem_dev), mem_dev), :] = piece
        else:
            turned[i] = piece
    for copy in first:
        copy.wait()
    mine = pl.ds(pl.multiple_of(z * mem_dev, mem_dev), mem_dev)
    total = part[bands + band]
    for i in range(1, bands):
        total = total + part[i]
    prior[band, mine, :] = total
    second = []
    for i in range(1, n_state):
        second.append(remote(prior.at[band, mine, :], prior.at[band, mine, :], s2.at[i], r2.at[i], {"state": z_peer(i)}))
        second[-1].start()
    inward = []
    for c in range(CHUNKS):
        rows = pl.ds(c * rows_chunk, rows_chunk)
        for i in range(1, n_state):
            inward.append(remote(turned.at[i, rows], fld.at[rows, mine, :], s_in.at[c, i], r_in.at[c, i], {"state": z_peer(i)}))
            inward[-1].start()

    my_block = (band * n_state + z).astype(f32)
    lane_cols = lax.broadcasted_iota(jnp.int32, (BATCH_OBS, col_dev), 1).astype(f32) + (z * col_dev).astype(f32)
    for b in range(BATCHES):
        o = pl.ds(b * BATCH_OBS, BATCH_OBS)
        row_w[b] = gap_weight(row_iota, lanes[2:3, o], rows_all)
        k_row, k_col = subs[o, 0:1], subs[o, 1:2]
        col_w[b] = gap_weight(lane_cols, k_col, cols_all)
        for later in range(b + 1, BATCHES):
            q = pl.ds(later * BATCH_OBS, BATCH_OBS)
            listed = subs[o, 2:3] == lanes[4:5, q]
            for l in range(1, n_list):
                listed = listed | (subs[o, 2 + l : 3 + l] == lanes[4:5, q])
            weight = gap_weight(k_row, lanes[2:3, q], rows_all) * gap_weight(k_col, lanes[3:4, q], cols_all)
            pair_w[b * BATCHES + later] = jnp.where(listed, weight, 0.0)

    for copy in second:
        copy.wait()
    third = []
    for i in range(1, bands):
        device, _ = band_peer(i)
        third.append(remote(prior.at[band], prior.at[band], s3.at[i], r3.at[i], device))
        third[-1].start()
    for copy in third:
        copy.wait()

    for b in range(BATCHES):
        o = pl.ds(b * BATCH_OBS, BATCH_OBS)
        x = prior[b]
        value, var = lanes[0:1, o], lanes[1:2, o]
        mean = jnp.mean(x, axis=0, keepdims=True)
        anom = x - mean
        spread = jnp.sum(anom * anom, axis=0, keepdims=True) / (members - 1) + 1e-06
        post_var = 1.0 / (1.0 / spread + 1.0 / var)
        post_mean = post_var * (mean / spread + value / var)
        shrink = jnp.sqrt(post_var / spread)
        scaled = (post_mean + shrink * anom - x) / ((members - 1) * spread)
        high, low = halves(anom)
        high = high.astype(f32)
        stacked = jnp.concatenate([high, high, low.astype(f32)], axis=0)
        left = stacked.T.astype(jnp.bfloat16)
        anom3[b] = left
        listed = lanes[5:6, o] == my_block
        for l in range(1, n_list):
            listed = listed | (lanes[5 + l : 6 + l, o] == my_block)
        step[b] = jnp.where(listed, scaled, 0.0)
        step_high, step_low = halves(scaled)
        both = jnp.concatenate([step_high, step_low], axis=0)
        for later in range(b + 1, BATCHES):
            y = prior[later]
            reg = dot32(left, split_anomaly(y)) * pair_w[b * BATCHES + later]
            reg_high, reg_low = halves(reg)
            big = dot32(both, reg_high)
            prior[later] = y + (big[:members] + (big[members:] + dot32(step_high, reg_low)))

    outward = []
    for c in range(CHUNKS):
        for copy in inward[c * (n_state - 1) : (c + 1) * (n_state - 1)]:
            copy.wait()

        def two_rows(p, carry, c=c):
            r = c * rows_chunk + 2 * p
            x = jnp.concatenate([fld[r], fld[r + 1]], axis=1)
            for b in range(BATCHES):
                cov = dot32(anom3[b], split_anomaly(x))
                adds = []
                for h in range(2):
                    reg = cov[:, h * col_dev : (h + 1) * col_dev] * col_w[b]
                    right = jnp.concatenate(halves(reg), axis=1)
                    left = jnp.concatenate(halves(step[b] * row_w[b, pl.ds(r + h, 1), :]), axis=0)
                    four = dot32(left, right)
                    adds.append(four[:members, :col_dev] + (four[:members, col_dev:] + four[members:, :col_dev]))
                x = x + jnp.concatenate(adds, axis=1)
            fld[r] = x[:, :col_dev]
            fld[r + 1] = x[:, col_dev:]
            return carry

        lax.fori_loop(0, rows_chunk // 2, two_rows, 0)
        rows = pl.ds(c * rows_chunk, rows_chunk)
        for i in range(1, n_state):
            d = z_peer(i)
            theirs = pl.ds(pl.multiple_of(d * mem_dev, mem_dev), mem_dev)
            outward.append(remote(fld.at[rows, theirs, :], back.at[i, rows], s_out.at[c, i], r_out.at[c, i], {"state": d}))
            outward[-1].start()
    out[:, :, pl.ds(pl.multiple_of(z * col_dev, col_dev), col_dev)] = jnp.swapaxes(fld[:, mine, :], 0, 1)
    for c in range(CHUNKS):
        rows = pl.ds(c * rows_chunk, rows_chunk)
        for i in range(1, n_state):
            outward[c * (n_state - 1) + i - 1].wait()
            s = lax.rem(z + n_state - i, n_state)
            out[:, rows, pl.ds(pl.multiple_of(s * col_dev, col_dev), col_dev)] = jnp.swapaxes(back[i, rows], 0, 1)


def fused(ensemble, value, var, obs_row, obs_col, obs_block, lists):
    n_state = lax.axis_size("state")
    n_cores = lax.axis_size("cores")
    mem_dev, row_dev, cols_all = ensemble.shape
    members = mem_dev * n_state
    col_dev = cols_all // n_state
    f32 = jnp.float32
    n_list = lists.shape[1]
    place = [obs_row.astype(f32), obs_col.astype(f32)]
    lanes = jnp.stack([value, var] + place + [obs_block.astype(f32)])
    lanes = jnp.concatenate([lanes, lists.astype(f32).T], axis=0)
    subs = jnp.concatenate([jnp.stack(place, axis=1), lists.astype(f32)], axis=1)
    vmem = pl.BlockSpec(memory_space=pltpu.VMEM)
    dma = pltpu.SemaphoreType.DMA
    return pl.pallas_call(
        functools.partial(kernel, n_state, n_cores, n_list),
        out_shape=jax.ShapeDtypeStruct(ensemble.shape, f32),
        in_specs=[vmem] * 3,
        out_specs=vmem,
        scratch_shapes=[
            pltpu.VMEM((n_state, row_dev, mem_dev, col_dev), f32),
            pltpu.VMEM((row_dev, members, col_dev), f32),
            pltpu.VMEM((n_state, row_dev, mem_dev, col_dev), f32),
            pltpu.VMEM((2 * BATCHES, mem_dev, BATCH_OBS), f32),
            pltpu.VMEM((BATCHES, members, BATCH_OBS), f32),
            pltpu.VMEM((BATCHES, BATCH_OBS, 3 * members), jnp.bfloat16),
            pltpu.VMEM((BATCHES, members, BATCH_OBS), f32),
            pltpu.VMEM((BATCHES, row_dev, BATCH_OBS), f32),
            pltpu.VMEM((BATCHES, BATCH_OBS, col_dev), f32),
            pltpu.VMEM((BATCHES * BATCHES, BATCH_OBS, BATCH_OBS), f32),
        ]
        + [dma((BATCHES,))] * 2
        + [dma((n_state,))] * 2
        + [dma((BATCHES,))] * 2
        + [dma((CHUNKS, n_state))] * 4,
        compiler_params=pltpu.CompilerParams(
            collective_id=0, has_side_effects=True, vmem_limit_bytes=40 * 2**20
        ),
    )(ensemble, lanes, subs)


def on_device(ensemble, obs_value, obs_var, obs_cell, obs_order, obs_blocks):
    n_state = lax.axis_size("state")
    n_obs = lax.axis_size("obs")
    n_cores = lax.axis_size("cores")
    mem_dev, row_dev, cols_all = ensemble.shape
    members = mem_dev * n_state
    col_dev = cols_all // n_state
    rows_all = row_dev * n_obs * n_cores
    row_band = lax.axis_index("obs") * n_cores + lax.axis_index("cores")
    row_start = row_band * row_dev
    col_start = lax.axis_index("state") * col_dev
    nobs = obs_order.shape[0]

    table = jnp.concatenate(
        [
            obs_value[:, None],
            obs_var[:, None],
            obs_cell.astype(jnp.float32)[:, None],
            obs_blocks.astype(jnp.float32),
        ],
        axis=1,
    )[obs_order]
    value, var = table[:, 0], table[:, 1]
    cells = table[:, 2].astype(jnp.int32)
    lists = table[:, 3:].astype(jnp.int32)
    obs_row = cells // cols_all
    obs_col = cells % cols_all
    obs_block = (obs_row // row_dev) * n_state + obs_col // col_dev

    if mem_dev % 8 == 0 and row_dev % CHUNKS == 0 and col_dev == 128 and n_obs * n_cores == BATCHES:
        return fused(ensemble, value, var, obs_row, obs_col, obs_block, lists)

    owned = (obs_row >= row_start) & (obs_row < row_start + row_dev)
    index = jnp.clip((obs_row - row_start) * cols_all + obs_col, 0, row_dev * cols_all - 1)
    mine = jnp.where(owned[None, :], ensemble.reshape(mem_dev, row_dev * cols_all)[:, index], 0.0)
    slot = jnp.zeros((members, nobs), jnp.float32)
    slot = lax.dynamic_update_slice_in_dim(slot, mine, lax.axis_index("state") * mem_dev, 0)
    at_obs = lax.psum(slot, ("state", "obs", "cores"))

    local_fields = lax.all_to_all(ensemble, "state", split_axis=2, concat_axis=0, tiled=True)
    count = row_dev * col_dev
    flat_index = jnp.arange(count, dtype=jnp.int32)
    cell_row = jnp.concatenate([row_start + flat_index // col_dev, obs_row])
    cell_col = jnp.concatenate([col_start + flat_index % col_dev, obs_col])
    my_block = row_band * n_state + lax.axis_index("state")
    cell_block = jnp.concatenate([jnp.full((count,), my_block, jnp.int32), obs_block])
    fields = jnp.concatenate([local_fields.reshape(members, count), at_obs], axis=1)
    for batch in range(BATCHES):
        part = slice(batch * BATCH_OBS, (batch + 1) * BATCH_OBS)
        prior_ens = fields[:, count + batch * BATCH_OBS : count + (batch + 1) * BATCH_OBS].T
        obs_anom, obs_step, obs_spread = adjust_obs(prior_ens, value[part], var[part])
        keep = count + nobs if batch < BATCHES - 1 else count
        listed = jnp.any(lists[part][:, :, None] == cell_block[None, None, :keep], axis=1)
        taper = distance_taper(
            obs_row[part], obs_col[part], cell_row[:keep], cell_col[:keep], rows_all, cols_all
        )
        taper_mask = jnp.where(listed, taper, 0.0)
        fields = fields[:, :keep]
        anomaly = fields - jnp.mean(fields, axis=0)
        covariance = jnp.dot(obs_anom, anomaly, precision=lax.Precision.HIGHEST) / (members - 1)
        regression = covariance * taper_mask / obs_spread[:, None]
        fields = fields + jnp.dot(obs_step.T, regression, precision=lax.Precision.HIGHEST)
    out_fields = fields.reshape(members, row_dev, col_dev)
    return lax.all_to_all(out_fields, "state", split_axis=0, concat_axis=2, tiled=True)


def solution(mesh):
    placed = (
        P(("groups", "state"), ("obs", "cores"), None),
        P("groups"),
        P("groups"),
        P("groups"),
        P("groups"),
        P("groups", None),
    )
    return jax.shard_map(
        on_device,
        mesh=mesh,
        in_specs=placed,
        out_specs=P(("groups", "state"), ("obs", "cores"), None),
        check_vma=False,
    )
```

```python
import functools
import jax
import jax.numpy as jnp
from jax import lax
from jax.experimental import pallas as pl
from jax.experimental.pallas import tpu as pltpu
from jax.sharding import PartitionSpec as P

BATCHES = 4
BATCH_OBS = 256
CHUNKS = 4


def adjust_obs(prior_ens, obs_value, obs_var):
    members = prior_ens.shape[1]
    ens_mean = jnp.mean(prior_ens, axis=1)
    obs_anom = prior_ens - ens_mean[:, None]
    obs_spread = jnp.sum(obs_anom * obs_anom, axis=1) / (members - 1) + 1e-06
    post_var = 1.0 / (1.0 / obs_spread + 1.0 / obs_var)
    post_mean = post_var * (ens_mean / obs_spread + obs_value / obs_var)
    shrink = jnp.sqrt(post_var / obs_spread)
    obs_step = post_mean[:, None] + shrink[:, None] * obs_anom - prior_ens
    return (obs_anom, obs_step, obs_spread)


def distance_taper(obs_row, obs_col, cell_row, cell_col, rows_all, cols_all):
    row_gap = jnp.abs(cell_row[None, :] - obs_row[:, None])
    row_gap = jnp.minimum(row_gap, rows_all - row_gap)
    col_gap = jnp.abs(cell_col[None, :] - obs_col[:, None])
    col_gap = jnp.minimum(col_gap, cols_all - col_gap)
    row_term = (4.0 * row_gap.astype(jnp.float32) / rows_all) ** 2
    col_term = (4.0 * col_gap.astype(jnp.float32) / cols_all) ** 2
    return jnp.exp(-0.5 * (row_term + col_term))


def halves(x):
    high = x.astype(jnp.bfloat16)
    return high, (x - high.astype(jnp.float32)).astype(jnp.bfloat16)


def thirds(x):
    high = x.astype(jnp.bfloat16)
    rest = x - high.astype(jnp.float32)
    mid = rest.astype(jnp.bfloat16)
    return high, mid, (rest - mid.astype(jnp.float32)).astype(jnp.bfloat16)


def dot32(a, b):
    return jnp.dot(a, b, preferred_element_type=jnp.float32)


def gap_weight(a, b, extent):
    gap = jnp.abs(a - b)
    gap = jnp.minimum(gap, extent - gap)
    term = gap * (4.0 / extent)
    return jnp.exp(-0.5 * (term * term))


def split_anomaly(x):
    high, low = halves(x - jnp.mean(x, axis=0, keepdims=True))
    return jnp.concatenate([high, low, high], axis=0)


def kernel(n_state, n_cores, n_list, ens, table, order, out, lanes, subs, turned, fld, back, part, prior,
           anom3, step, row_w, col_w, pair_w, s1, r1, s2, r2, s3, r3, s_in, r_in, s_out, r_out):
    mem_dev, row_dev, cols_all = ens.shape
    bands = BATCHES
    rows_all = row_dev * bands
    col_dev = cols_all // n_state
    members = mem_dev * n_state
    z = lax.axis_index("state")
    band = lax.axis_index("obs") * n_cores + lax.axis_index("cores")
    rows_chunk = row_dev // CHUNKS
    f32 = jnp.float32

    def z_peer(i):
        return lax.rem(z + i, n_state)

    def band_peer(i):
        p = lax.rem(band + i, bands)
        return {"obs": p // n_cores, "cores": lax.rem(p, n_cores)}, p

    def remote(src, dst, send, recv, device):
        return pltpu.make_async_remote_copy(
            src_ref=src, dst_ref=dst, send_sem=send, recv_sem=recv,
            device_id=device, device_id_type=pl.DeviceIdType.MESH,
        )

    barrier = pltpu.get_barrier_semaphore()
    for i in range(1, n_state):
        pl.semaphore_signal(barrier, inc=1, device_id={"state": z_peer(i)}, device_id_type=pl.DeviceIdType.MESH)
    for i in range(1, bands):
        pl.semaphore_signal(barrier, inc=1, device_id=band_peer(i)[0], device_id_type=pl.DeviceIdType.MESH)

    mine = pl.ds(pl.multiple_of(z * mem_dev, mem_dev), mem_dev)
    for i in range(n_state):
        d = z_peer(i)
        piece = jnp.swapaxes(ens[:, :, pl.ds(pl.multiple_of(d * col_dev, col_dev), col_dev)], 0, 1)
        if i == 0:
            fld[:, mine, :] = piece
        else:
            turned[i] = piece
    pl.semaphore_wait(barrier, n_state - 1 + bands - 1)
    inward = []

    def send_in(c):
        rows = pl.ds(c * rows_chunk, rows_chunk)
        for i in range(1, n_state):
            inward.append(remote(turned.at[i, rows], fld.at[rows, mine, :], s_in.at[c, i], r_in.at[c, i], {"state": z_peer(i)}))
            inward[-1].start()

    send_in(0)

    flat_table = jnp.concatenate(thirds(table[...]), axis=0)
    obs_iota = lax.broadcasted_iota(jnp.int32, (table.shape[1], BATCH_OBS), 0)
    height = table.shape[0]
    for b in range(BATCHES):
        o = pl.ds(b * BATCH_OBS, BATCH_OBS)
        onehot = jnp.where(obs_iota == order[0:1, o], 1.0, 0.0).astype(jnp.bfloat16)
        picked = dot32(flat_table, onehot)
        ordered = (picked[2 * height :] + picked[height : 2 * height]) + picked[:height]
        lanes[:, o] = ordered
        subs[o, :] = ordered.T

    flat = ens[...].reshape(mem_dev * row_dev, cols_all)
    high, mid, low = thirds(flat)
    col_iota = lax.broadcasted_iota(jnp.int32, (cols_all, BATCH_OBS), 0).astype(f32)
    row_iota = lax.broadcasted_iota(jnp.int32, (row_dev, BATCH_OBS), 0).astype(f32) + (band * row_dev).astype(f32)
    for b in range(BATCHES):
        o = pl.ds(b * BATCH_OBS, BATCH_OBS)
        onehot = jnp.where(col_iota == lanes[3:4, o], 1.0, 0.0).astype(jnp.bfloat16)
        picked = (dot32(low, onehot) + dot32(mid, onehot)) + dot32(high, onehot)
        mask = row_iota == lanes[2:3, o]
        picked = jnp.where(mask[None], picked.reshape(mem_dev, row_dev, BATCH_OBS), 0.0)
        part[bands + b] = jnp.sum(picked, axis=1)

    first = []
    for i in range(1, bands):
        device, p = band_peer(i)
        first.append(remote(part.at[bands + p], part.at[i], s1.at[i], r1.at[i], device))
        first[-1].start()
    for copy in first:
        copy.wait()
    total = part[bands + band]
    for i in range(1, bands):
        total = total + part[i]
    prior[band, mine, :] = total
    second = []
    for i in range(1, n_state):
        second.append(remote(prior.at[band, mine, :], prior.at[band, mine, :], s2.at[i], r2.at[i], {"state": z_peer(i)}))
        second[-1].start()
    for c in range(1, CHUNKS):
        send_in(c)

    my_block = (band * n_state + z).astype(f32)
    lane_cols = lax.broadcasted_iota(jnp.int32, (BATCH_OBS, col_dev), 1).astype(f32) + (z * col_dev).astype(f32)
    for b in range(BATCHES):
        o = pl.ds(b * BATCH_OBS, BATCH_OBS)
        row_w[b] = gap_weight(row_iota, lanes[2:3, o], rows_all)
        k_row, k_col = subs[o, 2:3], subs[o, 3:4]
        col_w[b] = gap_weight(lane_cols, k_col, cols_all)
        for later in range(b + 1, BATCHES):
            q = pl.ds(later * BATCH_OBS, BATCH_OBS)
            listed = subs[o, 5:6] == lanes[4:5, q]
            for l in range(1, n_list):
                listed = listed | (subs[o, 5 + l : 6 + l] == lanes[4:5, q])
            weight = gap_weight(k_row, lanes[2:3, q], rows_all) * gap_weight(k_col, lanes[3:4, q], cols_all)
            pair_w[b * BATCHES + later] = jnp.where(listed, weight, 0.0)

    for copy in second:
        copy.wait()
    third = []
    for i in range(1, bands):
        device, _ = band_peer(i)
        third.append(remote(prior.at[band], prior.at[band], s3.at[i], r3.at[i], device))
        third[-1].start()
    for copy in third:
        copy.wait()

    for b in range(BATCHES):
        o = pl.ds(b * BATCH_OBS, BATCH_OBS)
        x = prior[b]
        value, var = lanes[0:1, o], lanes[1:2, o]
        mean = jnp.mean(x, axis=0, keepdims=True)
        anom = x - mean
        spread = jnp.sum(anom * anom, axis=0, keepdims=True) / (members - 1) + 1e-06
        post_var = 1.0 / (1.0 / spread + 1.0 / var)
        post_mean = post_var * (mean / spread + value / var)
        shrink = jnp.sqrt(post_var / spread)
        scaled = (post_mean + shrink * anom - x) / ((members - 1) * spread)
        high, low = halves(anom)
        high = high.astype(f32)
        stacked = jnp.concatenate([high, high, low.astype(f32)], axis=0)
        left = stacked.T.astype(jnp.bfloat16)
        anom3[b] = left
        listed = lanes[5:6, o] == my_block
        for l in range(1, n_list):
            listed = listed | (lanes[5 + l : 6 + l, o] == my_block)
        step[b] = jnp.where(listed, scaled, 0.0)
        step_high, step_low = halves(scaled)
        both = jnp.concatenate([step_high, step_low], axis=0)
        for later in range(b + 1, BATCHES):
            y = prior[later]
            reg = dot32(left, split_anomaly(y)) * pair_w[b * BATCHES + later]
            reg_high, reg_low = halves(reg)
            big = dot32(both, reg_high)
            prior[later] = y + (big[:members] + (big[members:] + dot32(step_high, reg_low)))

    outward = []
    for c in range(CHUNKS):
        for copy in inward[c * (n_state - 1) : (c + 1) * (n_state - 1)]:
            copy.wait()

        def two_rows(p, carry, c=c):
            r = c * rows_chunk + 2 * p
            x = jnp.concatenate([fld[r], fld[r + 1]], axis=1)
            for b in range(BATCHES):
                cov = dot32(anom3[b], split_anomaly(x))
                adds = []
                for h in range(2):
                    reg = cov[:, h * col_dev : (h + 1) * col_dev] * col_w[b]
                    right = jnp.concatenate(halves(reg), axis=1)
                    left = jnp.concatenate(halves(step[b] * row_w[b, pl.ds(r + h, 1), :]), axis=0)
                    four = dot32(left, right)
                    adds.append(four[:members, :col_dev] + (four[:members, col_dev:] + four[members:, :col_dev]))
                x = x + jnp.concatenate(adds, axis=1)
            fld[r] = x[:, :col_dev]
            fld[r + 1] = x[:, col_dev:]
            return carry

        lax.fori_loop(0, rows_chunk // 2, two_rows, 0)
        rows = pl.ds(c * rows_chunk, rows_chunk)
        for i in range(1, n_state):
            d = z_peer(i)
            theirs = pl.ds(pl.multiple_of(d * mem_dev, mem_dev), mem_dev)
            outward.append(remote(fld.at[rows, theirs, :], back.at[i, rows], s_out.at[c, i], r_out.at[c, i], {"state": d}))
            outward[-1].start()
    out[:, :, pl.ds(pl.multiple_of(z * col_dev, col_dev), col_dev)] = jnp.swapaxes(fld[:, mine, :], 0, 1)
    for c in range(CHUNKS):
        rows = pl.ds(c * rows_chunk, rows_chunk)
        for i in range(1, n_state):
            outward[c * (n_state - 1) + i - 1].wait()
            s = lax.rem(z + n_state - i, n_state)
            out[:, rows, pl.ds(pl.multiple_of(s * col_dev, col_dev), col_dev)] = jnp.swapaxes(back[i, rows], 0, 1)


def fused(ensemble, obs_value, obs_var, obs_cell, obs_order, obs_blocks):
    n_state = lax.axis_size("state")
    n_cores = lax.axis_size("cores")
    mem_dev, row_dev, cols_all = ensemble.shape
    members = mem_dev * n_state
    col_dev = cols_all // n_state
    f32 = jnp.float32
    nobs, n_list = obs_blocks.shape
    height = -(-(5 + n_list) // 16) * 16
    row, col = obs_cell // cols_all, obs_cell % cols_all
    block = (row // row_dev) * n_state + col // col_dev
    table = jnp.stack([obs_value, obs_var, row.astype(f32), col.astype(f32), block.astype(f32)])
    spare = jnp.zeros((height - 5 - n_list, nobs), f32)
    table = jnp.concatenate([table, obs_blocks.astype(f32).T, spare], axis=0)
    vmem = pl.BlockSpec(memory_space=pltpu.VMEM)
    dma = pltpu.SemaphoreType.DMA
    return pl.pallas_call(
        functools.partial(kernel, n_state, n_cores, n_list),
        out_shape=jax.ShapeDtypeStruct(ensemble.shape, f32),
        in_specs=[vmem] * 3,
        out_specs=vmem,
        scratch_shapes=[
            pltpu.VMEM((height, nobs), f32),
            pltpu.VMEM((nobs, height), f32),
            pltpu.VMEM((n_state, row_dev, mem_dev, col_dev), f32),
            pltpu.VMEM((row_dev, members, col_dev), f32),
            pltpu.VMEM((n_state, row_dev, mem_dev, col_dev), f32),
            pltpu.VMEM((2 * BATCHES, mem_dev, BATCH_OBS), f32),
            pltpu.VMEM((BATCHES, members, BATCH_OBS), f32),
            pltpu.VMEM((BATCHES, BATCH_OBS, 3 * members), jnp.bfloat16),
            pltpu.VMEM((BATCHES, members, BATCH_OBS), f32),
            pltpu.VMEM((BATCHES, row_dev, BATCH_OBS), f32),
            pltpu.VMEM((BATCHES, BATCH_OBS, col_dev), f32),
            pltpu.VMEM((BATCHES * BATCHES, BATCH_OBS, BATCH_OBS), f32),
        ]
        + [dma((BATCHES,))] * 2
        + [dma((n_state,))] * 2
        + [dma((BATCHES,))] * 2
        + [dma((CHUNKS, n_state))] * 4,
        compiler_params=pltpu.CompilerParams(
            collective_id=0, has_side_effects=True, vmem_limit_bytes=40 * 2**20
        ),
    )(ensemble, table, obs_order.reshape(1, nobs))


def on_device(ensemble, obs_value, obs_var, obs_cell, obs_order, obs_blocks):
    n_state = lax.axis_size("state")
    n_obs = lax.axis_size("obs")
    n_cores = lax.axis_size("cores")
    mem_dev, row_dev, cols_all = ensemble.shape
    members = mem_dev * n_state
    col_dev = cols_all // n_state
    rows_all = row_dev * n_obs * n_cores
    row_band = lax.axis_index("obs") * n_cores + lax.axis_index("cores")
    row_start = row_band * row_dev
    col_start = lax.axis_index("state") * col_dev
    nobs = obs_order.shape[0]

    if mem_dev % 16 == 0 and row_dev % (2 * CHUNKS) == 0 and col_dev == 128 and n_obs * n_cores == BATCHES:
        return fused(ensemble, obs_value, obs_var, obs_cell, obs_order, obs_blocks)

    table = jnp.concatenate(
        [
            obs_value[:, None],
            obs_var[:, None],
            obs_cell.astype(jnp.float32)[:, None],
            obs_blocks.astype(jnp.float32),
        ],
        axis=1,
    )[obs_order]
    value, var = table[:, 0], table[:, 1]
    cells = table[:, 2].astype(jnp.int32)
    lists = table[:, 3:].astype(jnp.int32)
    obs_row = cells // cols_all
    obs_col = cells % cols_all
    obs_block = (obs_row // row_dev) * n_state + obs_col // col_dev

    owned = (obs_row >= row_start) & (obs_row < row_start + row_dev)
    index = jnp.clip((obs_row - row_start) * cols_all + obs_col, 0, row_dev * cols_all - 1)
    mine = jnp.where(owned[None, :], ensemble.reshape(mem_dev, row_dev * cols_all)[:, index], 0.0)
    slot = jnp.zeros((members, nobs), jnp.float32)
    slot = lax.dynamic_update_slice_in_dim(slot, mine, lax.axis_index("state") * mem_dev, 0)
    at_obs = lax.psum(slot, ("state", "obs", "cores"))

    local_fields = lax.all_to_all(ensemble, "state", split_axis=2, concat_axis=0, tiled=True)
    count = row_dev * col_dev
    flat_index = jnp.arange(count, dtype=jnp.int32)
    cell_row = jnp.concatenate([row_start + flat_index // col_dev, obs_row])
    cell_col = jnp.concatenate([col_start + flat_index % col_dev, obs_col])
    my_block = row_band * n_state + lax.axis_index("state")
    cell_block = jnp.concatenate([jnp.full((count,), my_block, jnp.int32), obs_block])
    fields = jnp.concatenate([local_fields.reshape(members, count), at_obs], axis=1)
    for batch in range(BATCHES):
        part = slice(batch * BATCH_OBS, (batch + 1) * BATCH_OBS)
        prior_ens = fields[:, count + batch * BATCH_OBS : count + (batch + 1) * BATCH_OBS].T
        obs_anom, obs_step, obs_spread = adjust_obs(prior_ens, value[part], var[part])
        keep = count + nobs if batch < BATCHES - 1 else count
        listed = jnp.any(lists[part][:, :, None] == cell_block[None, None, :keep], axis=1)
        taper = distance_taper(
            obs_row[part], obs_col[part], cell_row[:keep], cell_col[:keep], rows_all, cols_all
        )
        taper_mask = jnp.where(listed, taper, 0.0)
        fields = fields[:, :keep]
        anomaly = fields - jnp.mean(fields, axis=0)
        covariance = jnp.dot(obs_anom, anomaly, precision=lax.Precision.HIGHEST) / (members - 1)
        regression = covariance * taper_mask / obs_spread[:, None]
        fields = fields + jnp.dot(obs_step.T, regression, precision=lax.Precision.HIGHEST)
    out_fields = fields.reshape(members, row_dev, col_dev)
    return lax.all_to_all(out_fields, "state", split_axis=0, concat_axis=2, tiled=True)


def solution(mesh):
    placed = (
        P(("groups", "state"), ("obs", "cores"), None),
        P("groups"),
        P("groups"),
        P("groups"),
        P("groups"),
        P("groups", None),
    )
    return jax.shard_map(
        on_device,
        mesh=mesh,
        in_specs=placed,
        out_specs=P(("groups", "state"), ("obs", "cores"), None),
        check_vma=False,
    )
```

```python
import functools
import jax
import jax.numpy as jnp
from jax import lax
from jax.experimental import pallas as pl
from jax.experimental.pallas import tpu as pltpu
from jax.sharding import PartitionSpec as P

BATCHES = 4
BATCH_OBS = 256
CHUNKS = 4
PAIRS = 2


def adjust_obs(prior_ens, obs_value, obs_var):
    members = prior_ens.shape[1]
    ens_mean = jnp.mean(prior_ens, axis=1)
    obs_anom = prior_ens - ens_mean[:, None]
    obs_spread = jnp.sum(obs_anom * obs_anom, axis=1) / (members - 1) + 1e-06
    post_var = 1.0 / (1.0 / obs_spread + 1.0 / obs_var)
    post_mean = post_var * (ens_mean / obs_spread + obs_value / obs_var)
    shrink = jnp.sqrt(post_var / obs_spread)
    obs_step = post_mean[:, None] + shrink[:, None] * obs_anom - prior_ens
    return (obs_anom, obs_step, obs_spread)


def distance_taper(obs_row, obs_col, cell_row, cell_col, rows_all, cols_all):
    row_gap = jnp.abs(cell_row[None, :] - obs_row[:, None])
    row_gap = jnp.minimum(row_gap, rows_all - row_gap)
    col_gap = jnp.abs(cell_col[None, :] - obs_col[:, None])
    col_gap = jnp.minimum(col_gap, cols_all - col_gap)
    row_term = (4.0 * row_gap.astype(jnp.float32) / rows_all) ** 2
    col_term = (4.0 * col_gap.astype(jnp.float32) / cols_all) ** 2
    return jnp.exp(-0.5 * (row_term + col_term))


def halves(x):
    high = x.astype(jnp.bfloat16)
    return high, (x - high.astype(jnp.float32)).astype(jnp.bfloat16)


def thirds(x):
    high = x.astype(jnp.bfloat16)
    rest = x - high.astype(jnp.float32)
    mid = rest.astype(jnp.bfloat16)
    return high, mid, (rest - mid.astype(jnp.float32)).astype(jnp.bfloat16)


def dot32(a, b):
    return jnp.dot(a, b, preferred_element_type=jnp.float32)


def gap_weight(a, b, extent):
    gap = jnp.abs(a - b)
    gap = jnp.minimum(gap, extent - gap)
    term = gap * (4.0 / extent)
    return jnp.exp(-0.5 * (term * term))


def split_anomaly(x):
    high, low = halves(x - jnp.mean(x, axis=0, keepdims=True))
    return jnp.concatenate([high, low, high], axis=0)


def kernel(n_state, n_cores, n_list, ens, table, order, out, lanes, subs, turned, fld, back, part, prior,
           anom3, step, row_w, col_w, pair_w, s1, r1, s2, r2, s3, r3, s_in, r_in, s_out, r_out):
    mem_dev, row_dev, cols_all = ens.shape
    bands = BATCHES
    rows_all = row_dev * bands
    col_dev = cols_all // n_state
    members = mem_dev * n_state
    z = lax.axis_index("state")
    band = lax.axis_index("obs") * n_cores + lax.axis_index("cores")
    rows_chunk = row_dev // CHUNKS
    f32 = jnp.float32

    def z_peer(i):
        return lax.rem(z + i, n_state)

    def band_peer(i):
        p = lax.rem(band + i, bands)
        return {"obs": p // n_cores, "cores": lax.rem(p, n_cores)}, p

    def remote(src, dst, send, recv, device):
        return pltpu.make_async_remote_copy(
            src_ref=src, dst_ref=dst, send_sem=send, recv_sem=recv,
            device_id=device, device_id_type=pl.DeviceIdType.MESH,
        )

    barrier = pltpu.get_barrier_semaphore()
    for i in range(1, n_state):
        pl.semaphore_signal(barrier, inc=1, device_id={"state": z_peer(i)}, device_id_type=pl.DeviceIdType.MESH)
    for i in range(1, bands):
        pl.semaphore_signal(barrier, inc=1, device_id=band_peer(i)[0], device_id_type=pl.DeviceIdType.MESH)

    mine = pl.ds(pl.multiple_of(z * mem_dev, mem_dev), mem_dev)
    for i in range(n_state):
        d = z_peer(i)
        piece = jnp.swapaxes(ens[:, :, pl.ds(pl.multiple_of(d * col_dev, col_dev), col_dev)], 0, 1)
        if i == 0:
            fld[:, mine, :] = piece
        else:
            turned[i] = piece
    pl.semaphore_wait(barrier, n_state - 1 + bands - 1)
    inward = []

    def send_in(c):
        rows = pl.ds(c * rows_chunk, rows_chunk)
        for i in range(1, n_state):
            inward.append(remote(turned.at[i, rows], fld.at[rows, mine, :], s_in.at[c, i], r_in.at[c, i], {"state": z_peer(i)}))
            inward[-1].start()

    send_in(0)
    send_in(1)

    flat_table = jnp.concatenate(thirds(table[...]), axis=0)
    obs_iota = lax.broadcasted_iota(jnp.int32, (table.shape[1], BATCH_OBS), 0)
    height = table.shape[0]
    for b in range(BATCHES):
        o = pl.ds(b * BATCH_OBS, BATCH_OBS)
        onehot = jnp.where(obs_iota == order[0:1, o], 1.0, 0.0).astype(jnp.bfloat16)
        picked = dot32(flat_table, onehot)
        ordered = (picked[2 * height :] + picked[height : 2 * height]) + picked[:height]
        lanes[:, o] = ordered
        subs[o, :] = ordered.T

    flat = ens[...].reshape(mem_dev * row_dev, cols_all)
    high, mid, low = thirds(flat)
    col_iota = lax.broadcasted_iota(jnp.int32, (cols_all, BATCH_OBS), 0).astype(f32)
    row_iota = lax.broadcasted_iota(jnp.int32, (row_dev, BATCH_OBS), 0).astype(f32) + (band * row_dev).astype(f32)
    for b in range(BATCHES):
        o = pl.ds(b * BATCH_OBS, BATCH_OBS)
        onehot = jnp.where(col_iota == lanes[3:4, o], 1.0, 0.0).astype(jnp.bfloat16)
        picked = (dot32(low, onehot) + dot32(mid, onehot)) + dot32(high, onehot)
        mask = row_iota == lanes[2:3, o]
        picked = jnp.where(mask[None], picked.reshape(mem_dev, row_dev, BATCH_OBS), 0.0)
        part[bands + b] = jnp.sum(picked, axis=1)

    first = []
    for i in range(1, bands):
        device, p = band_peer(i)
        first.append(remote(part.at[bands + p], part.at[i], s1.at[i], r1.at[i], device))
        first[-1].start()
    for copy in first:
        copy.wait()
    total = part[bands + band]
    for i in range(1, bands):
        total = total + part[i]
    prior[band, mine, :] = total
    second = []
    for i in range(1, n_state):
        second.append(remote(prior.at[band, mine, :], prior.at[band, mine, :], s2.at[i], r2.at[i], {"state": z_peer(i)}))
        second[-1].start()
    for c in range(2, CHUNKS):
        send_in(c)

    my_block = (band * n_state + z).astype(f32)
    lane_cols = lax.broadcasted_iota(jnp.int32, (BATCH_OBS, col_dev), 1).astype(f32) + (z * col_dev).astype(f32)
    for b in range(BATCHES):
        o = pl.ds(b * BATCH_OBS, BATCH_OBS)
        row_w[b] = gap_weight(row_iota, lanes[2:3, o], rows_all)
        k_row, k_col = subs[o, 2:3], subs[o, 3:4]
        col_w[b] = gap_weight(lane_cols, k_col, cols_all)
        for later in range(b + 1, BATCHES):
            q = pl.ds(later * BATCH_OBS, BATCH_OBS)
            listed = subs[o, 5:6] == lanes[4:5, q]
            for l in range(1, n_list):
                listed = listed | (subs[o, 5 + l : 6 + l] == lanes[4:5, q])
            weight = gap_weight(k_row, lanes[2:3, q], rows_all) * gap_weight(k_col, lanes[3:4, q], cols_all)
            pair_w[b * BATCHES + later] = jnp.where(listed, weight, 0.0)

    for copy in second:
        copy.wait()
    third = []
    for i in range(1, bands):
        device, _ = band_peer(i)
        third.append(remote(prior.at[band], prior.at[band], s3.at[i], r3.at[i], device))
        third[-1].start()
    for copy in third:
        copy.wait()

    for b in range(BATCHES):
        o = pl.ds(b * BATCH_OBS, BATCH_OBS)
        x = prior[b]
        value, var = lanes[0:1, o], lanes[1:2, o]
        mean = jnp.mean(x, axis=0, keepdims=True)
        anom = x - mean
        spread = jnp.sum(anom * anom, axis=0, keepdims=True) / (members - 1) + 1e-06
        post_var = 1.0 / (1.0 / spread + 1.0 / var)
        post_mean = post_var * (mean / spread + value / var)
        shrink = jnp.sqrt(post_var / spread)
        scaled = (post_mean + shrink * anom - x) / ((members - 1) * spread)
        high, low = halves(anom)
        high = high.astype(f32)
        stacked = jnp.concatenate([high, high, low.astype(f32)], axis=0)
        left = stacked.T.astype(jnp.bfloat16)
        anom3[b] = left
        listed = lanes[5:6, o] == my_block
        for l in range(1, n_list):
            listed = listed | (lanes[5 + l : 6 + l, o] == my_block)
        step[b] = jnp.where(listed, scaled, 0.0)
        step_high, step_low = halves(scaled)
        both = jnp.concatenate([step_high, step_low], axis=0)
        for later in range(b + 1, BATCHES):
            y = prior[later]
            reg = dot32(left, split_anomaly(y)) * pair_w[b * BATCHES + later]
            reg_high, reg_low = halves(reg)
            big = dot32(both, reg_high)
            prior[later] = y + (big[:members] + (big[members:] + dot32(step_high, reg_low)))

    outward = []
    for c in range(CHUNKS):
        for copy in inward[c * (n_state - 1) : (c + 1) * (n_state - 1)]:
            copy.wait()

        def some_rows(p, carry, c=c):
            start = c * rows_chunk + 2 * PAIRS * p
            xs = [jnp.concatenate([fld[start + 2 * n], fld[start + 2 * n + 1]], axis=1) for n in range(PAIRS)]
            for b in range(BATCHES):
                covs = [dot32(anom3[b], split_anomaly(x)) for x in xs]
                for n in range(PAIRS):
                    adds = []
                    for h in range(2):
                        row = start + 2 * n + h
                        reg = covs[n][:, h * col_dev : (h + 1) * col_dev] * col_w[b]
                        right = jnp.concatenate(halves(reg), axis=1)
                        left = jnp.concatenate(halves(step[b] * row_w[b, pl.ds(row, 1), :]), axis=0)
                        four = dot32(left, right)
                        adds.append(four[:members, :col_dev] + (four[:members, col_dev:] + four[members:, :col_dev]))
                    xs[n] = xs[n] + jnp.concatenate(adds, axis=1)
            for n in range(PAIRS):
                fld[start + 2 * n] = xs[n][:, :col_dev]
                fld[start + 2 * n + 1] = xs[n][:, col_dev:]
            return carry

        lax.fori_loop(0, rows_chunk // (2 * PAIRS), some_rows, 0)
        rows = pl.ds(c * rows_chunk, rows_chunk)
        for i in range(1, n_state):
            d = z_peer(i)
            theirs = pl.ds(pl.multiple_of(d * mem_dev, mem_dev), mem_dev)
            outward.append(remote(fld.at[rows, theirs, :], back.at[i, rows], s_out.at[c, i], r_out.at[c, i], {"state": d}))
            outward[-1].start()
    out[:, :, pl.ds(pl.multiple_of(z * col_dev, col_dev), col_dev)] = jnp.swapaxes(fld[:, mine, :], 0, 1)
    for c in range(CHUNKS):
        rows = pl.ds(c * rows_chunk, rows_chunk)
        for i in range(1, n_state):
            outward[c * (n_state - 1) + i - 1].wait()
            s = lax.rem(z + n_state - i, n_state)
            out[:, rows, pl.ds(pl.multiple_of(s * col_dev, col_dev), col_dev)] = jnp.swapaxes(back[i, rows], 0, 1)


def fused(ensemble, obs_value, obs_var, obs_cell, obs_order, obs_blocks):
    n_state = lax.axis_size("state")
    n_cores = lax.axis_size("cores")
    mem_dev, row_dev, cols_all = ensemble.shape
    members = mem_dev * n_state
    col_dev = cols_all // n_state
    f32 = jnp.float32
    nobs, n_list = obs_blocks.shape
    height = -(-(5 + n_list) // 16) * 16
    row, col = obs_cell // cols_all, obs_cell % cols_all
    block = (row // row_dev) * n_state + col // col_dev
    table = jnp.stack([obs_value, obs_var, row.astype(f32), col.astype(f32), block.astype(f32)])
    spare = jnp.zeros((height - 5 - n_list, nobs), f32)
    table = jnp.concatenate([table, obs_blocks.astype(f32).T, spare], axis=0)
    vmem = pl.BlockSpec(memory_space=pltpu.VMEM)
    dma = pltpu.SemaphoreType.DMA
    return pl.pallas_call(
        functools.partial(kernel, n_state, n_cores, n_list),
        out_shape=jax.ShapeDtypeStruct(ensemble.shape, f32),
        in_specs=[vmem] * 3,
        out_specs=vmem,
        scratch_shapes=[
            pltpu.VMEM((height, nobs), f32),
            pltpu.VMEM((nobs, height), f32),
            pltpu.VMEM((n_state, row_dev, mem_dev, col_dev), f32),
            pltpu.VMEM((row_dev, members, col_dev), f32),
            pltpu.VMEM((n_state, row_dev, mem_dev, col_dev), f32),
            pltpu.VMEM((2 * BATCHES, mem_dev, BATCH_OBS), f32),
            pltpu.VMEM((BATCHES, members, BATCH_OBS), f32),
            pltpu.VMEM((BATCHES, BATCH_OBS, 3 * members), jnp.bfloat16),
            pltpu.VMEM((BATCHES, members, BATCH_OBS), f32),
            pltpu.VMEM((BATCHES, row_dev, BATCH_OBS), f32),
            pltpu.VMEM((BATCHES, BATCH_OBS, col_dev), f32),
            pltpu.VMEM((BATCHES * BATCHES, BATCH_OBS, BATCH_OBS), f32),
        ]
        + [dma((BATCHES,))] * 2
        + [dma((n_state,))] * 2
        + [dma((BATCHES,))] * 2
        + [dma((CHUNKS, n_state))] * 4,
        compiler_params=pltpu.CompilerParams(
            collective_id=0, has_side_effects=True, vmem_limit_bytes=40 * 2**20
        ),
    )(ensemble, table, obs_order.reshape(1, nobs))


def on_device(ensemble, obs_value, obs_var, obs_cell, obs_order, obs_blocks):
    n_state = lax.axis_size("state")
    n_obs = lax.axis_size("obs")
    n_cores = lax.axis_size("cores")
    mem_dev, row_dev, cols_all = ensemble.shape
    members = mem_dev * n_state
    col_dev = cols_all // n_state
    rows_all = row_dev * n_obs * n_cores
    row_band = lax.axis_index("obs") * n_cores + lax.axis_index("cores")
    row_start = row_band * row_dev
    col_start = lax.axis_index("state") * col_dev
    nobs = obs_order.shape[0]

    if mem_dev % 16 == 0 and row_dev % (2 * PAIRS * CHUNKS) == 0 and col_dev == 128 and n_obs * n_cores == BATCHES:
        return fused(ensemble, obs_value, obs_var, obs_cell, obs_order, obs_blocks)

    table = jnp.concatenate(
        [
            obs_value[:, None],
            obs_var[:, None],
            obs_cell.astype(jnp.float32)[:, None],
            obs_blocks.astype(jnp.float32),
        ],
        axis=1,
    )[obs_order]
    value, var = table[:, 0], table[:, 1]
    cells = table[:, 2].astype(jnp.int32)
    lists = table[:, 3:].astype(jnp.int32)
    obs_row = cells // cols_all
    obs_col = cells % cols_all
    obs_block = (obs_row // row_dev) * n_state + obs_col // col_dev

    owned = (obs_row >= row_start) & (obs_row < row_start + row_dev)
    index = jnp.clip((obs_row - row_start) * cols_all + obs_col, 0, row_dev * cols_all - 1)
    mine = jnp.where(owned[None, :], ensemble.reshape(mem_dev, row_dev * cols_all)[:, index], 0.0)
    slot = jnp.zeros((members, nobs), jnp.float32)
    slot = lax.dynamic_update_slice_in_dim(slot, mine, lax.axis_index("state") * mem_dev, 0)
    at_obs = lax.psum(slot, ("state", "obs", "cores"))

    local_fields = lax.all_to_all(ensemble, "state", split_axis=2, concat_axis=0, tiled=True)
    count = row_dev * col_dev
    flat_index = jnp.arange(count, dtype=jnp.int32)
    cell_row = jnp.concatenate([row_start + flat_index // col_dev, obs_row])
    cell_col = jnp.concatenate([col_start + flat_index % col_dev, obs_col])
    my_block = row_band * n_state + lax.axis_index("state")
    cell_block = jnp.concatenate([jnp.full((count,), my_block, jnp.int32), obs_block])
    fields = jnp.concatenate([local_fields.reshape(members, count), at_obs], axis=1)
    for batch in range(BATCHES):
        part = slice(batch * BATCH_OBS, (batch + 1) * BATCH_OBS)
        prior_ens = fields[:, count + batch * BATCH_OBS : count + (batch + 1) * BATCH_OBS].T
        obs_anom, obs_step, obs_spread = adjust_obs(prior_ens, value[part], var[part])
        keep = count + nobs if batch < BATCHES - 1 else count
        listed = jnp.any(lists[part][:, :, None] == cell_block[None, None, :keep], axis=1)
        taper = distance_taper(
            obs_row[part], obs_col[part], cell_row[:keep], cell_col[:keep], rows_all, cols_all
        )
        taper_mask = jnp.where(listed, taper, 0.0)
        fields = fields[:, :keep]
        anomaly = fields - jnp.mean(fields, axis=0)
        covariance = jnp.dot(obs_anom, anomaly, precision=lax.Precision.HIGHEST) / (members - 1)
        regression = covariance * taper_mask / obs_spread[:, None]
        fields = fields + jnp.dot(obs_step.T, regression, precision=lax.Precision.HIGHEST)
    out_fields = fields.reshape(members, row_dev, col_dev)
    return lax.all_to_all(out_fields, "state", split_axis=0, concat_axis=2, tiled=True)


def solution(mesh):
    placed = (
        P(("groups", "state"), ("obs", "cores"), None),
        P("groups"),
        P("groups"),
        P("groups"),
        P("groups"),
        P("groups", None),
    )
    return jax.shard_map(
        on_device,
        mesh=mesh,
        in_specs=placed,
        out_specs=P(("groups", "state"), ("obs", "cores"), None),
        check_vma=False,
    )
```

```python
import functools
import jax
import jax.numpy as jnp
from jax import lax
from jax.experimental import pallas as pl
from jax.experimental.pallas import tpu as pltpu
from jax.sharding import PartitionSpec as P

BATCHES = 4
BATCH_OBS = 256
CHUNKS = 8
PAIRS = 2


def adjust_obs(prior_ens, obs_value, obs_var):
    members = prior_ens.shape[1]
    ens_mean = jnp.mean(prior_ens, axis=1)
    obs_anom = prior_ens - ens_mean[:, None]
    obs_spread = jnp.sum(obs_anom * obs_anom, axis=1) / (members - 1) + 1e-06
    post_var = 1.0 / (1.0 / obs_spread + 1.0 / obs_var)
    post_mean = post_var * (ens_mean / obs_spread + obs_value / obs_var)
    shrink = jnp.sqrt(post_var / obs_spread)
    obs_step = post_mean[:, None] + shrink[:, None] * obs_anom - prior_ens
    return (obs_anom, obs_step, obs_spread)


def distance_taper(obs_row, obs_col, cell_row, cell_col, rows_all, cols_all):
    row_gap = jnp.abs(cell_row[None, :] - obs_row[:, None])
    row_gap = jnp.minimum(row_gap, rows_all - row_gap)
    col_gap = jnp.abs(cell_col[None, :] - obs_col[:, None])
    col_gap = jnp.minimum(col_gap, cols_all - col_gap)
    row_term = (4.0 * row_gap.astype(jnp.float32) / rows_all) ** 2
    col_term = (4.0 * col_gap.astype(jnp.float32) / cols_all) ** 2
    return jnp.exp(-0.5 * (row_term + col_term))


def halves(x):
    high = x.astype(jnp.bfloat16)
    return high, (x - high.astype(jnp.float32)).astype(jnp.bfloat16)


def thirds(x):
    high = x.astype(jnp.bfloat16)
    rest = x - high.astype(jnp.float32)
    mid = rest.astype(jnp.bfloat16)
    return high, mid, (rest - mid.astype(jnp.float32)).astype(jnp.bfloat16)


def dot32(a, b):
    return jnp.dot(a, b, preferred_element_type=jnp.float32)


def gap_weight(a, b, extent):
    gap = jnp.abs(a - b)
    gap = jnp.minimum(gap, extent - gap)
    term = gap * (4.0 / extent)
    return jnp.exp(-0.5 * (term * term))


def split_anomaly(x):
    high, low = halves(x - jnp.mean(x, axis=0, keepdims=True))
    return jnp.concatenate([high, low, high], axis=0)


def kernel(n_state, n_cores, n_list, ens, table, order, out, lanes, subs, turned, fld, back, part, prior,
           anom3, step, row_w, col_w, pair_w, s1, r1, s2, r2, s3, r3, s_in, r_in, s_out, r_out):
    mem_dev, row_dev, cols_all = ens.shape
    bands = BATCHES
    rows_all = row_dev * bands
    col_dev = cols_all // n_state
    members = mem_dev * n_state
    z = lax.axis_index("state")
    band = lax.axis_index("obs") * n_cores + lax.axis_index("cores")
    rows_chunk = row_dev // CHUNKS
    f32 = jnp.float32

    def z_peer(i):
        return lax.rem(z + i, n_state)

    def band_peer(i):
        p = lax.rem(band + i, bands)
        return {"obs": p // n_cores, "cores": lax.rem(p, n_cores)}, p

    def remote(src, dst, send, recv, device):
        return pltpu.make_async_remote_copy(
            src_ref=src, dst_ref=dst, send_sem=send, recv_sem=recv,
            device_id=device, device_id_type=pl.DeviceIdType.MESH,
        )

    barrier = pltpu.get_barrier_semaphore()
    for i in range(1, n_state):
        pl.semaphore_signal(barrier, inc=1, device_id={"state": z_peer(i)}, device_id_type=pl.DeviceIdType.MESH)
    for i in range(1, bands):
        pl.semaphore_signal(barrier, inc=1, device_id=band_peer(i)[0], device_id_type=pl.DeviceIdType.MESH)

    mine = pl.ds(pl.multiple_of(z * mem_dev, mem_dev), mem_dev)
    for i in range(n_state):
        d = z_peer(i)
        piece = jnp.swapaxes(ens[:, :, pl.ds(pl.multiple_of(d * col_dev, col_dev), col_dev)], 0, 1)
        if i == 0:
            fld[:, mine, :] = piece
        else:
            turned[i] = piece
    pl.semaphore_wait(barrier, n_state - 1 + bands - 1)
    inward = []

    def send_in(c):
        rows = pl.ds(c * rows_chunk, rows_chunk)
        for i in range(1, n_state):
            inward.append(remote(turned.at[i, rows], fld.at[rows, mine, :], s_in.at[c, i], r_in.at[c, i], {"state": z_peer(i)}))
            inward[-1].start()

    send_in(0)
    send_in(1)

    flat_table = jnp.concatenate(thirds(table[...]), axis=0)
    obs_iota = lax.broadcasted_iota(jnp.int32, (table.shape[1], BATCH_OBS), 0)
    height = table.shape[0]
    for b in range(BATCHES):
        o = pl.ds(b * BATCH_OBS, BATCH_OBS)
        onehot = jnp.where(obs_iota == order[0:1, o], 1.0, 0.0).astype(jnp.bfloat16)
        picked = dot32(flat_table, onehot)
        ordered = (picked[2 * height :] + picked[height : 2 * height]) + picked[:height]
        lanes[:, o] = ordered
        subs[o, :] = ordered.T

    flat = ens[...].reshape(mem_dev * row_dev, cols_all)
    high, mid, low = thirds(flat)
    col_iota = lax.broadcasted_iota(jnp.int32, (cols_all, BATCH_OBS), 0).astype(f32)
    row_iota = lax.broadcasted_iota(jnp.int32, (row_dev, BATCH_OBS), 0).astype(f32) + (band * row_dev).astype(f32)
    for b in range(BATCHES):
        o = pl.ds(b * BATCH_OBS, BATCH_OBS)
        onehot = jnp.where(col_iota == lanes[3:4, o], 1.0, 0.0).astype(jnp.bfloat16)
        picked = (dot32(low, onehot) + dot32(mid, onehot)) + dot32(high, onehot)
        mask = row_iota == lanes[2:3, o]
        picked = jnp.where(mask[None], picked.reshape(mem_dev, row_dev, BATCH_OBS), 0.0)
        part[bands + b] = jnp.sum(picked, axis=1)

    first = []
    for i in range(1, bands):
        device, p = band_peer(i)
        first.append(remote(part.at[bands + p], part.at[i], s1.at[i], r1.at[i], device))
        first[-1].start()
    for copy in first:
        copy.wait()
    total = part[bands + band]
    for i in range(1, bands):
        total = total + part[i]
    prior[band, mine, :] = total
    second = []
    for i in range(1, n_state):
        second.append(remote(prior.at[band, mine, :], prior.at[band, mine, :], s2.at[i], r2.at[i], {"state": z_peer(i)}))
        second[-1].start()
    for c in range(2, CHUNKS):
        send_in(c)

    my_block = (band * n_state + z).astype(f32)
    lane_cols = lax.broadcasted_iota(jnp.int32, (BATCH_OBS, col_dev), 1).astype(f32) + (z * col_dev).astype(f32)
    for b in range(BATCHES):
        o = pl.ds(b * BATCH_OBS, BATCH_OBS)
        row_w[b] = gap_weight(row_iota, lanes[2:3, o], rows_all)
        k_row, k_col = subs[o, 2:3], subs[o, 3:4]
        col_w[b] = gap_weight(lane_cols, k_col, cols_all)
        for later in range(b + 1, BATCHES):
            q = pl.ds(later * BATCH_OBS, BATCH_OBS)
            listed = subs[o, 5:6] == lanes[4:5, q]
            for l in range(1, n_list):
                listed = listed | (subs[o, 5 + l : 6 + l] == lanes[4:5, q])
            weight = gap_weight(k_row, lanes[2:3, q], rows_all) * gap_weight(k_col, lanes[3:4, q], cols_all)
            pair_w[b * BATCHES + later] = jnp.where(listed, weight, 0.0)

    for copy in second:
        copy.wait()
    third = []
    for i in range(1, bands):
        device, _ = band_peer(i)
        third.append(remote(prior.at[band], prior.at[band], s3.at[i], r3.at[i], device))
        third[-1].start()
    for copy in third:
        copy.wait()

    for b in range(BATCHES):
        o = pl.ds(b * BATCH_OBS, BATCH_OBS)
        x = prior[b]
        value, var = lanes[0:1, o], lanes[1:2, o]
        mean = jnp.mean(x, axis=0, keepdims=True)
        anom = x - mean
        spread = jnp.sum(anom * anom, axis=0, keepdims=True) / (members - 1) + 1e-06
        post_var = 1.0 / (1.0 / spread + 1.0 / var)
        post_mean = post_var * (mean / spread + value / var)
        shrink = jnp.sqrt(post_var / spread)
        scaled = (post_mean + shrink * anom - x) / ((members - 1) * spread)
        high, low = halves(anom)
        high = high.astype(f32)
        stacked = jnp.concatenate([high, high, low.astype(f32)], axis=0)
        left = stacked.T.astype(jnp.bfloat16)
        anom3[b] = left
        listed = lanes[5:6, o] == my_block
        for l in range(1, n_list):
            listed = listed | (lanes[5 + l : 6 + l, o] == my_block)
        step[b] = jnp.where(listed, scaled, 0.0)
        step_high, step_low = halves(scaled)
        both = jnp.concatenate([step_high, step_low], axis=0)
        for later in range(b + 1, BATCHES):
            y = prior[later]
            reg = dot32(left, split_anomaly(y)) * pair_w[b * BATCHES + later]
            reg_high, reg_low = halves(reg)
            big = dot32(both, reg_high)
            prior[later] = y + (big[:members] + (big[members:] + dot32(step_high, reg_low)))

    outward = []
    for c in range(CHUNKS):
        for copy in inward[c * (n_state - 1) : (c + 1) * (n_state - 1)]:
            copy.wait()

        def some_rows(p, carry, c=c):
            start = c * rows_chunk + 2 * PAIRS * p
            xs = [jnp.concatenate([fld[start + 2 * n], fld[start + 2 * n + 1]], axis=1) for n in range(PAIRS)]
            for b in range(BATCHES):
                covs = [dot32(anom3[b], split_anomaly(x)) for x in xs]
                for n in range(PAIRS):
                    adds = []
                    for h in range(2):
                        row = start + 2 * n + h
                        reg = covs[n][:, h * col_dev : (h + 1) * col_dev] * col_w[b]
                        right = jnp.concatenate(halves(reg), axis=1)
                        left = jnp.concatenate(halves(step[b] * row_w[b, pl.ds(row, 1), :]), axis=0)
                        four = dot32(left, right)
                        adds.append(four[:members, :col_dev] + (four[:members, col_dev:] + four[members:, :col_dev]))
                    xs[n] = xs[n] + jnp.concatenate(adds, axis=1)
            for n in range(PAIRS):
                fld[start + 2 * n] = xs[n][:, :col_dev]
                fld[start + 2 * n + 1] = xs[n][:, col_dev:]
            return carry

        lax.fori_loop(0, rows_chunk // (2 * PAIRS), some_rows, 0)
        rows = pl.ds(c * rows_chunk, rows_chunk)
        for i in range(1, n_state):
            d = z_peer(i)
            theirs = pl.ds(pl.multiple_of(d * mem_dev, mem_dev), mem_dev)
            outward.append(remote(fld.at[rows, theirs, :], back.at[i, rows], s_out.at[c, i], r_out.at[c, i], {"state": d}))
            outward[-1].start()
    out[:, :, pl.ds(pl.multiple_of(z * col_dev, col_dev), col_dev)] = jnp.swapaxes(fld[:, mine, :], 0, 1)
    for c in range(0, CHUNKS, 2):
        rows = pl.ds(c * rows_chunk, 2 * rows_chunk)
        for i in range(1, n_state):
            outward[c * (n_state - 1) + i - 1].wait()
            outward[(c + 1) * (n_state - 1) + i - 1].wait()
            s = lax.rem(z + n_state - i, n_state)
            out[:, rows, pl.ds(pl.multiple_of(s * col_dev, col_dev), col_dev)] = jnp.swapaxes(back[i, rows], 0, 1)


def fused(ensemble, obs_value, obs_var, obs_cell, obs_order, obs_blocks):
    n_state = lax.axis_size("state")
    n_cores = lax.axis_size("cores")
    mem_dev, row_dev, cols_all = ensemble.shape
    members = mem_dev * n_state
    col_dev = cols_all // n_state
    f32 = jnp.float32
    nobs, n_list = obs_blocks.shape
    height = -(-(5 + n_list) // 16) * 16
    row, col = obs_cell // cols_all, obs_cell % cols_all
    block = (row // row_dev) * n_state + col // col_dev
    table = jnp.stack([obs_value, obs_var, row.astype(f32), col.astype(f32), block.astype(f32)])
    spare = jnp.zeros((height - 5 - n_list, nobs), f32)
    table = jnp.concatenate([table, obs_blocks.astype(f32).T, spare], axis=0)
    vmem = pl.BlockSpec(memory_space=pltpu.VMEM)
    dma = pltpu.SemaphoreType.DMA
    return pl.pallas_call(
        functools.partial(kernel, n_state, n_cores, n_list),
        out_shape=jax.ShapeDtypeStruct(ensemble.shape, f32),
        in_specs=[vmem] * 3,
        out_specs=vmem,
        scratch_shapes=[
            pltpu.VMEM((height, nobs), f32),
            pltpu.VMEM((nobs, height), f32),
            pltpu.VMEM((n_state, row_dev, mem_dev, col_dev), f32),
            pltpu.VMEM((row_dev, members, col_dev), f32),
            pltpu.VMEM((n_state, row_dev, mem_dev, col_dev), f32),
            pltpu.VMEM((2 * BATCHES, mem_dev, BATCH_OBS), f32),
            pltpu.VMEM((BATCHES, members, BATCH_OBS), f32),
            pltpu.VMEM((BATCHES, BATCH_OBS, 3 * members), jnp.bfloat16),
            pltpu.VMEM((BATCHES, members, BATCH_OBS), f32),
            pltpu.VMEM((BATCHES, row_dev, BATCH_OBS), f32),
            pltpu.VMEM((BATCHES, BATCH_OBS, col_dev), f32),
            pltpu.VMEM((BATCHES * BATCHES, BATCH_OBS, BATCH_OBS), f32),
        ]
        + [dma((BATCHES,))] * 2
        + [dma((n_state,))] * 2
        + [dma((BATCHES,))] * 2
        + [dma((CHUNKS, n_state))] * 4,
        compiler_params=pltpu.CompilerParams(
            collective_id=0, has_side_effects=True, vmem_limit_bytes=40 * 2**20
        ),
    )(ensemble, table, obs_order.reshape(1, nobs))


def on_device(ensemble, obs_value, obs_var, obs_cell, obs_order, obs_blocks):
    n_state = lax.axis_size("state")
    n_obs = lax.axis_size("obs")
    n_cores = lax.axis_size("cores")
    mem_dev, row_dev, cols_all = ensemble.shape
    members = mem_dev * n_state
    col_dev = cols_all // n_state
    rows_all = row_dev * n_obs * n_cores
    row_band = lax.axis_index("obs") * n_cores + lax.axis_index("cores")
    row_start = row_band * row_dev
    col_start = lax.axis_index("state") * col_dev
    nobs = obs_order.shape[0]

    if mem_dev % 16 == 0 and row_dev % (2 * PAIRS * CHUNKS) == 0 and col_dev == 128 and n_obs * n_cores == BATCHES:
        return fused(ensemble, obs_value, obs_var, obs_cell, obs_order, obs_blocks)

    table = jnp.concatenate(
        [
            obs_value[:, None],
            obs_var[:, None],
            obs_cell.astype(jnp.float32)[:, None],
            obs_blocks.astype(jnp.float32),
        ],
        axis=1,
    )[obs_order]
    value, var = table[:, 0], table[:, 1]
    cells = table[:, 2].astype(jnp.int32)
    lists = table[:, 3:].astype(jnp.int32)
    obs_row = cells // cols_all
    obs_col = cells % cols_all
    obs_block = (obs_row // row_dev) * n_state + obs_col // col_dev

    owned = (obs_row >= row_start) & (obs_row < row_start + row_dev)
    index = jnp.clip((obs_row - row_start) * cols_all + obs_col, 0, row_dev * cols_all - 1)
    mine = jnp.where(owned[None, :], ensemble.reshape(mem_dev, row_dev * cols_all)[:, index], 0.0)
    slot = jnp.zeros((members, nobs), jnp.float32)
    slot = lax.dynamic_update_slice_in_dim(slot, mine, lax.axis_index("state") * mem_dev, 0)
    at_obs = lax.psum(slot, ("state", "obs", "cores"))

    local_fields = lax.all_to_all(ensemble, "state", split_axis=2, concat_axis=0, tiled=True)
    count = row_dev * col_dev
    flat_index = jnp.arange(count, dtype=jnp.int32)
    cell_row = jnp.concatenate([row_start + flat_index // col_dev, obs_row])
    cell_col = jnp.concatenate([col_start + flat_index % col_dev, obs_col])
    my_block = row_band * n_state + lax.axis_index("state")
    cell_block = jnp.concatenate([jnp.full((count,), my_block, jnp.int32), obs_block])
    fields = jnp.concatenate([local_fields.reshape(members, count), at_obs], axis=1)
    for batch in range(BATCHES):
        part = slice(batch * BATCH_OBS, (batch + 1) * BATCH_OBS)
        prior_ens = fields[:, count + batch * BATCH_OBS : count + (batch + 1) * BATCH_OBS].T
        obs_anom, obs_step, obs_spread = adjust_obs(prior_ens, value[part], var[part])
        keep = count + nobs if batch < BATCHES - 1 else count
        listed = jnp.any(lists[part][:, :, None] == cell_block[None, None, :keep], axis=1)
        taper = distance_taper(
            obs_row[part], obs_col[part], cell_row[:keep], cell_col[:keep], rows_all, cols_all
        )
        taper_mask = jnp.where(listed, taper, 0.0)
        fields = fields[:, :keep]
        anomaly = fields - jnp.mean(fields, axis=0)
        covariance = jnp.dot(obs_anom, anomaly, precision=lax.Precision.HIGHEST) / (members - 1)
        regression = covariance * taper_mask / obs_spread[:, None]
        fields = fields + jnp.dot(obs_step.T, regression, precision=lax.Precision.HIGHEST)
    out_fields = fields.reshape(members, row_dev, col_dev)
    return lax.all_to_all(out_fields, "state", split_axis=0, concat_axis=2, tiled=True)


def solution(mesh):
    placed = (
        P(("groups", "state"), ("obs", "cores"), None),
        P("groups"),
        P("groups"),
        P("groups"),
        P("groups"),
        P("groups", None),
    )
    return jax.shard_map(
        on_device,
        mesh=mesh,
        in_specs=placed,
        out_specs=P(("groups", "state"), ("obs", "cores"), None),
        check_vma=False,
    )
```

```python
import functools
import jax
import jax.numpy as jnp
from jax import lax
from jax.experimental import pallas as pl
from jax.experimental.pallas import tpu as pltpu
from jax.sharding import PartitionSpec as P

BATCHES = 4
BATCH_OBS = 256
CHUNKS = 8
PAIRS = 2


def adjust_obs(prior_ens, obs_value, obs_var):
    members = prior_ens.shape[1]
    ens_mean = jnp.mean(prior_ens, axis=1)
    obs_anom = prior_ens - ens_mean[:, None]
    obs_spread = jnp.sum(obs_anom * obs_anom, axis=1) / (members - 1) + 1e-06
    post_var = 1.0 / (1.0 / obs_spread + 1.0 / obs_var)
    post_mean = post_var * (ens_mean / obs_spread + obs_value / obs_var)
    shrink = jnp.sqrt(post_var / obs_spread)
    obs_step = post_mean[:, None] + shrink[:, None] * obs_anom - prior_ens
    return (obs_anom, obs_step, obs_spread)


def distance_taper(obs_row, obs_col, cell_row, cell_col, rows_all, cols_all):
    row_gap = jnp.abs(cell_row[None, :] - obs_row[:, None])
    row_gap = jnp.minimum(row_gap, rows_all - row_gap)
    col_gap = jnp.abs(cell_col[None, :] - obs_col[:, None])
    col_gap = jnp.minimum(col_gap, cols_all - col_gap)
    row_term = (4.0 * row_gap.astype(jnp.float32) / rows_all) ** 2
    col_term = (4.0 * col_gap.astype(jnp.float32) / cols_all) ** 2
    return jnp.exp(-0.5 * (row_term + col_term))


def halves(x):
    high = x.astype(jnp.bfloat16)
    return high, (x - high.astype(jnp.float32)).astype(jnp.bfloat16)


def thirds(x):
    high = x.astype(jnp.bfloat16)
    rest = x - high.astype(jnp.float32)
    mid = rest.astype(jnp.bfloat16)
    return high, mid, (rest - mid.astype(jnp.float32)).astype(jnp.bfloat16)


def dot32(a, b):
    return jnp.dot(a, b, preferred_element_type=jnp.float32)


def gap_weight(a, b, extent):
    gap = jnp.abs(a - b)
    gap = jnp.minimum(gap, extent - gap)
    term = gap * (4.0 / extent)
    return jnp.exp(-0.5 * (term * term))


def split_anomaly(x):
    high, low = halves(x - jnp.mean(x, axis=0, keepdims=True))
    return jnp.concatenate([high, low, high], axis=0)


def kernel(n_state, n_cores, n_list, ens, table, order, out, lanes, subs, turned, fld, back, part, prior,
           anom3, step, row_w, col_w, pair_w, s1, r1, s2, r2, s3, r3, s_in, r_in, s_out, r_out):
    mem_dev, row_dev, cols_all = ens.shape
    bands = BATCHES
    rows_all = row_dev * bands
    col_dev = cols_all // n_state
    members = mem_dev * n_state
    z = lax.axis_index("state")
    band = lax.axis_index("obs") * n_cores + lax.axis_index("cores")
    rows_chunk = row_dev // CHUNKS
    f32 = jnp.float32

    def z_peer(i):
        return lax.rem(z + i, n_state)

    def band_peer(i):
        p = lax.rem(band + i, bands)
        return {"obs": p // n_cores, "cores": lax.rem(p, n_cores)}, p

    def remote(src, dst, send, recv, device):
        return pltpu.make_async_remote_copy(
            src_ref=src, dst_ref=dst, send_sem=send, recv_sem=recv,
            device_id=device, device_id_type=pl.DeviceIdType.MESH,
        )

    barrier = pltpu.get_barrier_semaphore()
    for i in range(1, n_state):
        pl.semaphore_signal(barrier, inc=1, device_id={"state": z_peer(i)}, device_id_type=pl.DeviceIdType.MESH)
    for i in range(1, bands):
        pl.semaphore_signal(barrier, inc=1, device_id=band_peer(i)[0], device_id_type=pl.DeviceIdType.MESH)

    mine = pl.ds(pl.multiple_of(z * mem_dev, mem_dev), mem_dev)
    for i in range(n_state):
        d = z_peer(i)
        piece = jnp.swapaxes(ens[:, :, pl.ds(pl.multiple_of(d * col_dev, col_dev), col_dev)], 0, 1)
        if i == 0:
            fld[:, mine, :] = piece
        else:
            turned[i] = piece
    pl.semaphore_wait(barrier, n_state - 1 + bands - 1)
    inward = []

    def send_in(c):
        rows = pl.ds(c * rows_chunk, rows_chunk)
        for i in range(1, n_state):
            inward.append(remote(turned.at[i, rows], fld.at[rows, mine, :], s_in.at[c, i], r_in.at[c, i], {"state": z_peer(i)}))
            inward[-1].start()

    send_in(0)

    flat_table = jnp.concatenate(thirds(table[...]), axis=0)
    obs_iota = lax.broadcasted_iota(jnp.int32, (table.shape[1], BATCH_OBS), 0)
    height = table.shape[0]
    for b in range(BATCHES):
        o = pl.ds(b * BATCH_OBS, BATCH_OBS)
        onehot = jnp.where(obs_iota == order[0:1, o], 1.0, 0.0).astype(jnp.bfloat16)
        picked = dot32(flat_table, onehot)
        ordered = (picked[2 * height :] + picked[height : 2 * height]) + picked[:height]
        lanes[:, o] = ordered
        subs[o, :] = ordered.T

    flat = ens[...].reshape(mem_dev * row_dev, cols_all)
    high, mid, low = thirds(flat)
    col_iota = lax.broadcasted_iota(jnp.int32, (cols_all, BATCH_OBS), 0).astype(f32)
    row_iota = lax.broadcasted_iota(jnp.int32, (row_dev, BATCH_OBS), 0).astype(f32) + (band * row_dev).astype(f32)
    for b in range(BATCHES):
        o = pl.ds(b * BATCH_OBS, BATCH_OBS)
        onehot = jnp.where(col_iota == lanes[3:4, o], 1.0, 0.0).astype(jnp.bfloat16)
        picked = (dot32(low, onehot) + dot32(mid, onehot)) + dot32(high, onehot)
        mask = row_iota == lanes[2:3, o]
        picked = jnp.where(mask[None], picked.reshape(mem_dev, row_dev, BATCH_OBS), 0.0)
        part[bands + b] = jnp.sum(picked, axis=1)

    first = []
    for i in range(1, bands):
        device, p = band_peer(i)
        first.append(remote(part.at[bands + p], part.at[i], s1.at[i], r1.at[i], device))
        first[-1].start()
    for copy in first:
        copy.wait()
    total = part[bands + band]
    for i in range(1, bands):
        total = total + part[i]
    prior[band, mine, :] = total
    second = []
    for i in range(1, n_state):
        second.append(remote(prior.at[band, mine, :], prior.at[band, mine, :], s2.at[i], r2.at[i], {"state": z_peer(i)}))
        second[-1].start()
    for c in range(1, CHUNKS):
        send_in(c)

    my_block = (band * n_state + z).astype(f32)
    lane_cols = lax.broadcasted_iota(jnp.int32, (BATCH_OBS, col_dev), 1).astype(f32) + (z * col_dev).astype(f32)
    for b in range(BATCHES):
        o = pl.ds(b * BATCH_OBS, BATCH_OBS)
        row_w[b] = gap_weight(row_iota, lanes[2:3, o], rows_all)
        k_row, k_col = subs[o, 2:3], subs[o, 3:4]
        col_w[b] = gap_weight(lane_cols, k_col, cols_all)
        for later in range(b + 1, BATCHES):
            q = pl.ds(later * BATCH_OBS, BATCH_OBS)
            listed = subs[o, 5:6] == lanes[4:5, q]
            for l in range(1, n_list):
                listed = listed | (subs[o, 5 + l : 6 + l] == lanes[4:5, q])
            weight = gap_weight(k_row, lanes[2:3, q], rows_all) * gap_weight(k_col, lanes[3:4, q], cols_all)
            pair_w[b * BATCHES + later] = jnp.where(listed, weight, 0.0)

    for copy in second:
        copy.wait()
    third = []
    for i in range(1, bands):
        device, _ = band_peer(i)
        third.append(remote(prior.at[band], prior.at[band], s3.at[i], r3.at[i], device))
        third[-1].start()
    for copy in third:
        copy.wait()

    for b in range(BATCHES):
        o = pl.ds(b * BATCH_OBS, BATCH_OBS)
        x = prior[b]
        value, var = lanes[0:1, o], lanes[1:2, o]
        mean = jnp.mean(x, axis=0, keepdims=True)
        anom = x - mean
        spread = jnp.sum(anom * anom, axis=0, keepdims=True) / (members - 1) + 1e-06
        post_var = 1.0 / (1.0 / spread + 1.0 / var)
        post_mean = post_var * (mean / spread + value / var)
        shrink = jnp.sqrt(post_var / spread)
        scaled = (post_mean + shrink * anom - x) / ((members - 1) * spread)
        high, low = halves(anom)
        high = high.astype(f32)
        stacked = jnp.concatenate([high, high, low.astype(f32)], axis=0)
        left = stacked.T.astype(jnp.bfloat16)
        anom3[b] = left
        listed = lanes[5:6, o] == my_block
        for l in range(1, n_list):
            listed = listed | (lanes[5 + l : 6 + l, o] == my_block)
        step[b] = jnp.where(listed, scaled, 0.0)
        step_high, step_low = halves(scaled)
        both = jnp.concatenate([step_high, step_low], axis=0)
        for later in range(b + 1, BATCHES):
            y = prior[later]
            reg = dot32(left, split_anomaly(y)) * pair_w[b * BATCHES + later]
            reg_high, reg_low = halves(reg)
            big = dot32(both, reg_high)
            prior[later] = y + (big[:members] + (big[members:] + dot32(step_high, reg_low)))

    outward = []
    for c in range(CHUNKS):
        for copy in inward[c * (n_state - 1) : (c + 1) * (n_state - 1)]:
            copy.wait()

        def some_rows(p, carry, c=c):
            start = c * rows_chunk + 2 * PAIRS * p
            xs = [jnp.concatenate([fld[start + 2 * n], fld[start + 2 * n + 1]], axis=1) for n in range(PAIRS)]
            for b in range(BATCHES):
                covs = [dot32(anom3[b], split_anomaly(x)) for x in xs]
                for n in range(PAIRS):
                    adds = []
                    for h in range(2):
                        row = start + 2 * n + h
                        reg = covs[n][:, h * col_dev : (h + 1) * col_dev] * col_w[b]
                        right = jnp.concatenate(halves(reg), axis=1)
                        left = jnp.concatenate(halves(step[b] * row_w[b, pl.ds(row, 1), :]), axis=0)
                        four = dot32(left, right)
                        adds.append(four[:members, :col_dev] + (four[:members, col_dev:] + four[members:, :col_dev]))
                    xs[n] = xs[n] + jnp.concatenate(adds, axis=1)
            for n in range(PAIRS):
                fld[start + 2 * n] = xs[n][:, :col_dev]
                fld[start + 2 * n + 1] = xs[n][:, col_dev:]
            return carry

        lax.fori_loop(0, rows_chunk // (2 * PAIRS), some_rows, 0)
        rows = pl.ds(c * rows_chunk, rows_chunk)
        for i in range(1, n_state):
            d = z_peer(i)
            theirs = pl.ds(pl.multiple_of(d * mem_dev, mem_dev), mem_dev)
            outward.append(remote(fld.at[rows, theirs, :], back.at[i, rows], s_out.at[c, i], r_out.at[c, i], {"state": d}))
            outward[-1].start()
    out[:, :, pl.ds(pl.multiple_of(z * col_dev, col_dev), col_dev)] = jnp.swapaxes(fld[:, mine, :], 0, 1)
    for c in range(0, CHUNKS, 2):
        rows = pl.ds(c * rows_chunk, 2 * rows_chunk)
        for i in range(1, n_state):
            outward[c * (n_state - 1) + i - 1].wait()
            outward[(c + 1) * (n_state - 1) + i - 1].wait()
            s = lax.rem(z + n_state - i, n_state)
            out[:, rows, pl.ds(pl.multiple_of(s * col_dev, col_dev), col_dev)] = jnp.swapaxes(back[i, rows], 0, 1)


def fused(ensemble, obs_value, obs_var, obs_cell, obs_order, obs_blocks):
    n_state = lax.axis_size("state")
    n_cores = lax.axis_size("cores")
    mem_dev, row_dev, cols_all = ensemble.shape
    members = mem_dev * n_state
    col_dev = cols_all // n_state
    f32 = jnp.float32
    nobs, n_list = obs_blocks.shape
    height = -(-(5 + n_list) // 16) * 16
    row, col = obs_cell // cols_all, obs_cell % cols_all
    block = (row // row_dev) * n_state + col // col_dev
    table = jnp.stack([obs_value, obs_var, row.astype(f32), col.astype(f32), block.astype(f32)])
    spare = jnp.zeros((height - 5 - n_list, nobs), f32)
    table = jnp.concatenate([table, obs_blocks.astype(f32).T, spare], axis=0)
    vmem = pl.BlockSpec(memory_space=pltpu.VMEM)
    dma = pltpu.SemaphoreType.DMA
    return pl.pallas_call(
        functools.partial(kernel, n_state, n_cores, n_list),
        out_shape=jax.ShapeDtypeStruct(ensemble.shape, f32),
        in_specs=[vmem] * 3,
        out_specs=vmem,
        scratch_shapes=[
            pltpu.VMEM((height, nobs), f32),
            pltpu.VMEM((nobs, height), f32),
            pltpu.VMEM((n_state, row_dev, mem_dev, col_dev), f32),
            pltpu.VMEM((row_dev, members, col_dev), f32),
            pltpu.VMEM((n_state, row_dev, mem_dev, col_dev), f32),
            pltpu.VMEM((2 * BATCHES, mem_dev, BATCH_OBS), f32),
            pltpu.VMEM((BATCHES, members, BATCH_OBS), f32),
            pltpu.VMEM((BATCHES, BATCH_OBS, 3 * members), jnp.bfloat16),
            pltpu.VMEM((BATCHES, members, BATCH_OBS), f32),
            pltpu.VMEM((BATCHES, row_dev, BATCH_OBS), f32),
            pltpu.VMEM((BATCHES, BATCH_OBS, col_dev), f32),
            pltpu.VMEM((BATCHES * BATCHES, BATCH_OBS, BATCH_OBS), f32),
        ]
        + [dma((BATCHES,))] * 2
        + [dma((n_state,))] * 2
        + [dma((BATCHES,))] * 2
        + [dma((CHUNKS, n_state))] * 4,
        compiler_params=pltpu.CompilerParams(
            collective_id=0, has_side_effects=True, vmem_limit_bytes=40 * 2**20
        ),
    )(ensemble, table, obs_order.reshape(1, nobs))


def on_device(ensemble, obs_value, obs_var, obs_cell, obs_order, obs_blocks):
    n_state = lax.axis_size("state")
    n_obs = lax.axis_size("obs")
    n_cores = lax.axis_size("cores")
    mem_dev, row_dev, cols_all = ensemble.shape
    members = mem_dev * n_state
    col_dev = cols_all // n_state
    rows_all = row_dev * n_obs * n_cores
    row_band = lax.axis_index("obs") * n_cores + lax.axis_index("cores")
    row_start = row_band * row_dev
    col_start = lax.axis_index("state") * col_dev
    nobs = obs_order.shape[0]

    if mem_dev % 16 == 0 and row_dev % (2 * PAIRS * CHUNKS) == 0 and col_dev == 128 and n_obs * n_cores == BATCHES:
        return fused(ensemble, obs_value, obs_var, obs_cell, obs_order, obs_blocks)

    table = jnp.concatenate(
        [
            obs_value[:, None],
            obs_var[:, None],
            obs_cell.astype(jnp.float32)[:, None],
            obs_blocks.astype(jnp.float32),
        ],
        axis=1,
    )[obs_order]
    value, var = table[:, 0], table[:, 1]
    cells = table[:, 2].astype(jnp.int32)
    lists = table[:, 3:].astype(jnp.int32)
    obs_row = cells // cols_all
    obs_col = cells % cols_all
    obs_block = (obs_row // row_dev) * n_state + obs_col // col_dev

    owned = (obs_row >= row_start) & (obs_row < row_start + row_dev)
    index = jnp.clip((obs_row - row_start) * cols_all + obs_col, 0, row_dev * cols_all - 1)
    mine = jnp.where(owned[None, :], ensemble.reshape(mem_dev, row_dev * cols_all)[:, index], 0.0)
    slot = jnp.zeros((members, nobs), jnp.float32)
    slot = lax.dynamic_update_slice_in_dim(slot, mine, lax.axis_index("state") * mem_dev, 0)
    at_obs = lax.psum(slot, ("state", "obs", "cores"))

    local_fields = lax.all_to_all(ensemble, "state", split_axis=2, concat_axis=0, tiled=True)
    count = row_dev * col_dev
    flat_index = jnp.arange(count, dtype=jnp.int32)
    cell_row = jnp.concatenate([row_start + flat_index // col_dev, obs_row])
    cell_col = jnp.concatenate([col_start + flat_index % col_dev, obs_col])
    my_block = row_band * n_state + lax.axis_index("state")
    cell_block = jnp.concatenate([jnp.full((count,), my_block, jnp.int32), obs_block])
    fields = jnp.concatenate([local_fields.reshape(members, count), at_obs], axis=1)
    for batch in range(BATCHES):
        part = slice(batch * BATCH_OBS, (batch + 1) * BATCH_OBS)
        prior_ens = fields[:, count + batch * BATCH_OBS : count + (batch + 1) * BATCH_OBS].T
        obs_anom, obs_step, obs_spread = adjust_obs(prior_ens, value[part], var[part])
        keep = count + nobs if batch < BATCHES - 1 else count
        listed = jnp.any(lists[part][:, :, None] == cell_block[None, None, :keep], axis=1)
        taper = distance_taper(
            obs_row[part], obs_col[part], cell_row[:keep], cell_col[:keep], rows_all, cols_all
        )
        taper_mask = jnp.where(listed, taper, 0.0)
        fields = fields[:, :keep]
        anomaly = fields - jnp.mean(fields, axis=0)
        covariance = jnp.dot(obs_anom, anomaly, precision=lax.Precision.HIGHEST) / (members - 1)
        regression = covariance * taper_mask / obs_spread[:, None]
        fields = fields + jnp.dot(obs_step.T, regression, precision=lax.Precision.HIGHEST)
    out_fields = fields.reshape(members, row_dev, col_dev)
    return lax.all_to_all(out_fields, "state", split_axis=0, concat_axis=2, tiled=True)


def solution(mesh):
    placed = (
        P(("groups", "state"), ("obs", "cores"), None),
        P("groups"),
        P("groups"),
        P("groups"),
        P("groups"),
        P("groups", None),
    )
    return jax.shard_map(
        on_device,
        mesh=mesh,
        in_specs=placed,
        out_specs=P(("groups", "state"), ("obs", "cores"), None),
        check_vma=False,
    )
```
